512 devices in a mesh: group: 8 (over z_hi, core), rows: 64 (over z_lo, x, y).
Axes of the slice: x: 4, y: 8, z: 8 (z_hi: 4, z_lo: 2; z = z_hi * 2 + z_lo), core: 2. Of those that a mesh axis runs over, the one named last changes fastest.
Arguments:
- illum_tilts: int32 [8, 2], P('group'), may hold values from -430 to 430
- index_layers: float32 [1, 2048, 2048], P(None, 'rows', 'group'), may hold values from -0.02 to 0.02
- measured: float32 [8, 2, 2048, 2048], P('group', None, 'rows'), may hold values from -4 to 4
Outputs:
- residual: float32 [8, 2, 2048, 2048], P('group', None, 'rows')
The draws below stay inside these ranges and needn't reach their ends.
All inputs are finite; a program needn't handle non-finite values.
Results may differ from the reference program's by a relative error of at most 0.0003.
Values sent between devices are 32-bit elements; how exact they have to be, the bound alone decides.
A program may use at most 64 MiB of HBM per device.

```python
import math
import jax
import jax.numpy as jnp
from jax import lax

N = 2048
LAYERS = 1
ILLUMS = 8


def set_ends(entries, rng, smallest, largest):
    shape = entries.shape
    place = [jax.random.randint(jax.random.fold_in(rng, axis), (), 0, shape[axis]) for axis in range(len(shape))]
    entries = entries.at[tuple(place)].set(smallest)
    longest = shape.index(max(shape))
    place[longest] = (place[longest] + 1) % shape[longest]
    return entries.at[tuple(place)].set(largest)


def block_scale(rng, shape, pieces, low, largest):
    def one(dim, shards_of):
        steps = jax.random.uniform(jax.random.fold_in(jax.random.fold_in(rng, 6), dim), (shards_of,), jnp.float32, low / len(pieces), largest / len(pieces))
        return jnp.repeat(jnp.exp(steps), shape[dim] // shards_of).reshape((-1,) + (1,) * (len(shape) - dim - 1))

    factor_of = one(*pieces[0])
    for cut in pieces[1:]:
        factor_of = factor_of * one(*cut)
    return factor_of


def gaussian(key, dims, spread, reach, pieces=(), held_as=jnp.bfloat16):
    values = spread * jax.random.normal(key, dims, jnp.float32)
    if pieces:
        values = values * block_scale(key, dims, pieces, -0.22, 0.18)
    return jnp.clip(values, -reach, reach).astype(held_as)


def setup_inputs(seed: int = 0) -> dict:
    keys = jax.random.split(jax.random.key(seed), 4)
    return {
        "illum_tilts": set_ends(jax.random.randint(keys[0], (ILLUMS, 2), -(N * 21 // 100), N * 21 // 100 + 1), jax.random.fold_in(keys[0], 1), -(N * 21 // 100), (N * 21 // 100 + 1) - 1).astype(jnp.int32),
        "index_layers": jnp.clip(jax.random.uniform(keys[1], (LAYERS, N, N), jnp.float32, -0.02, 0.02) * block_scale(keys[1], (LAYERS, N, N), ((1, 64), (2, 8)), -0.4, 0.0), -0.02, 0.02),
        "measured": gaussian(keys[2], (ILLUMS, 2, N, N), 0.5, 4.0, ((0, 8), (2, 64)), jnp.float32),
    }


THICKNESS = 4.0

def signed_freqs(extent):
    steps = jnp.arange(extent, dtype=jnp.int32)
    return jnp.where(steps < extent // 2, steps, steps - extent)

def pupil_parts(freq_rows, freq_cols):
    radius = freq_rows * freq_rows + freq_cols * freq_cols
    inside = 100 * radius < 9 * N * N
    radius_norm = radius.astype(jnp.float32) / float((N // 2) ** 2)
    axial_root = jnp.sqrt(1.0 - jnp.minimum(radius_norm, 0.36))
    phase_angle = 2.0 * math.pi * THICKNESS * (axial_root - 1.0)
    inside_mask = inside.astype(jnp.float32)
    return (inside_mask * jnp.cos(phase_angle), inside_mask * jnp.sin(phase_angle))

def incident_wave(tilt_pair):
    row_pos = jnp.arange(N, dtype=jnp.int32)[:, None]
    col_pos = jnp.arange(N, dtype=jnp.int32)[None, :]
    residue = jnp.mod(tilt_pair[0] * row_pos + tilt_pair[1] * col_pos, N)
    phase_angle = residue.astype(jnp.float32) * (2.0 * math.pi / N)
    return (jnp.cos(phase_angle), jnp.sin(phase_angle))

def reference(illum_tilts, index_layers, measured):
    freqs = signed_freqs(N)
    pupil_real, pupil_imag = pupil_parts(freqs[:, None], freqs[None, :])
    aperture = lax.complex(pupil_real, pupil_imag)

    def propagate_one(sample):
        tilt_pair, observed = sample
        wave_real, wave_imag = incident_wave(tilt_pair)
        wave_field = lax.complex(wave_real, wave_imag)
        for layer_step in range(LAYERS):
            phase_angle = 2.0 * math.pi * THICKNESS * index_layers[layer_step]
            wave_field = wave_field * lax.complex(jnp.cos(phase_angle), jnp.sin(phase_angle))
            wave_field = jnp.fft.ifft2(jnp.fft.fft2(wave_field) * aperture)
        return jnp.stack([jnp.real(wave_field) - observed[0], jnp.imag(wave_field) - observed[1]])
    return lax.map(propagate_one, (illum_tilts, measured))
```

```python
import math

import jax
import jax.numpy as jnp
import ml_dtypes
import numpy as np
from jax import lax
from jax.experimental import pallas as pl
from jax.experimental.pallas import tpu as pltpu
from jax.sharding import PartitionSpec as P

N = 2048
THICKNESS = 4.0
MESH = pl.DeviceIdType.MESH

GROUPS = 8
ROWS = 64
STRIP = N // ROWS
LOW = 16
HIGH = 128
BANDS = 80
SUB = 5
FOLD = 4
MSG = 2 * SUB
TILES = LOW // FOLD
SLOTS = BANDS // SUB


def split_const(table):
    high = table.astype(ml_dtypes.bfloat16)
    low = (table - high.astype(np.float64)).astype(ml_dtypes.bfloat16)
    return high, low


def real_form(cosine, sine, order="out_in"):
    return np.block([[cosine, -sine], [sine, cosine]])


def tables():
    two_pi = 2.0 * math.pi
    m = np.arange(BANDS) - BANDS // 2
    angle = two_pi * ((m[:, None] * np.arange(HIGH)[None, :]) % HIGH) / HIGH
    forward = real_form(np.cos(angle), -np.sin(angle)).reshape(2, SLOTS, SUB, 2 * HIGH)
    col_fwd = forward.transpose(1, 0, 2, 3).reshape(2 * BANDS, 2 * HIGH)
    inverse = real_form(np.cos(angle.T), np.sin(angle.T)).reshape(2 * HIGH, 2, SLOTS, SUB)
    col_inv = inverse.transpose(2, 1, 3, 0).reshape(2 * BANDS, 2 * HIGH)
    step = np.arange(ROWS)
    angle = two_pi * ((step[:, None] * step[None, :]) % ROWS) / ROWS
    row_fwd = real_form(np.cos(angle), -np.sin(angle))
    row_inv = real_form(np.cos(angle), np.sin(angle))
    step = np.arange(STRIP)
    angle = two_pi * ((step[:, None] * step[None, :]) % STRIP) / STRIP
    eye = np.eye(FOLD)
    cosine, sine = np.kron(eye, np.cos(angle)), np.kron(eye, np.sin(angle))
    in_fwd = real_form(cosine, -sine).T
    in_inv = real_form(cosine, sine).T
    angle = two_pi * (np.arange(LOW)[:, None] * np.arange(HIGH)[None, :]) / N
    col_twist = np.stack([np.cos(angle), np.sin(angle)]).astype(np.float32)
    angle = two_pi * (np.arange(ROWS)[:, None] * np.arange(STRIP)[None, :]) / N
    row_twist = np.stack([np.tile(np.cos(angle), FOLD), np.tile(np.sin(angle), FOLD)]).astype(
        np.float32
    )
    wide = np.stack(split_const(np.concatenate([col_fwd, col_inv, in_fwd, in_inv])))
    narrow = np.stack(split_const(np.concatenate([row_fwd, row_inv])))
    return wide, narrow, col_twist, row_twist


COL_FWD = (0, 2 * BANDS)
COL_INV = (2 * BANDS, 2 * BANDS)
IN_FWD = (4 * BANDS, 2 * HIGH)
IN_INV = (4 * BANDS + 2 * HIGH, 2 * HIGH)
ROW_FWD = (0, 2 * ROWS)
ROW_INV = (2 * ROWS, 2 * ROWS)


def sincos_cycles(cycles):
    cycles = cycles - jnp.round(cycles)
    quarter = cycles * (0.5 * math.pi)
    square = quarter * quarter
    sine = quarter * (
        1.0 + square * (-1.0 / 6 + square * (1.0 / 120 + square * (-1.0 / 5040 + square * (1.0 / 362880))))
    )
    cosine = 1.0 + square * (
        -0.5 + square * (1.0 / 24 + square * (-1.0 / 720 + square * (1.0 / 40320 - square * (1.0 / 3628800))))
    )
    sine, cosine = 2.0 * sine * cosine, 1.0 - 2.0 * sine * sine
    sine, cosine = 2.0 * sine * cosine, 1.0 - 2.0 * sine * sine
    return cosine, sine


def sincos_small(angle):
    square = angle * angle
    sine = angle * (1.0 + square * (-1.0 / 6 + square * (1.0 / 120 - square * (1.0 / 5040))))
    cosine = 1.0 + square * (-0.5 + square * (1.0 / 24 + square * (-1.0 / 720 + square * (1.0 / 40320))))
    return cosine, sine


def cmul(a, b):
    return (a[0] * b[0] - a[1] * b[1], a[0] * b[1] + a[1] * b[0])


def cadd(a, b):
    return (a[0] + b[0], a[1] + b[1])


def csub(a, b):
    return (a[0] - b[0], a[1] - b[1])


def dft4(a, sign):
    even, odd = cadd(a[0], a[2]), cadd(a[1], a[3])
    even_d, odd_d = csub(a[0], a[2]), csub(a[1], a[3])
    turned = (-odd_d[1], odd_d[0]) if sign > 0 else (odd_d[1], -odd_d[0])
    return [cadd(even, odd), cadd(even_d, turned), csub(even, odd), csub(even_d, turned)]


def dft16(v, sign):
    half = math.sqrt(0.5)
    firsts = [dft4([v[4 * n1 + n2] for n1 in range(4)], sign) for n2 in range(4)]
    out = [None] * 16
    for k1 in range(4):
        column = []
        for n2 in range(4):
            re, im = firsts[n2][k1]
            turn = n2 * k1
            if turn == 2:
                re, im = (
                    (half * (re - im), half * (re + im)) if sign > 0 else (half * (re + im), half * (im - re))
                )
            elif turn == 4:
                re, im = (-im, re) if sign > 0 else (im, -re)
            elif turn == 6:
                re, im = (
                    (-half * (re + im), half * (re - im)) if sign > 0 else (half * (im - re), -half * (re + im))
                )
            elif turn:
                angle = 2.0 * math.pi * turn / 16
                re, im = cmul((re, im), (math.cos(angle), sign * math.sin(angle)))
            column.append((re, im))
        for k2, value in enumerate(dft4(column, sign)):
            out[k1 + 4 * k2] = value
    return out


def split(value):
    high = value.astype(jnp.bfloat16)
    low = (value - high.astype(jnp.float32)).astype(jnp.bfloat16)
    return high, low


def dot3(a, b, dims):
    def one(x, y):
        return lax.dot_general(x, y, (dims, ((), ())), preferred_element_type=jnp.float32)

    return one(a[0], b[0]) + (one(a[0], b[1]) + one(a[1], b[0]))


def pupil_parts(freq_rows, freq_cols):
    radius = freq_rows * freq_rows + freq_cols * freq_cols
    inside = 100 * radius < 9 * N * N
    radius_norm = radius.astype(jnp.float32) * (1.0 / float((N // 2) ** 2))
    axial_root = jnp.sqrt(1.0 - jnp.minimum(radius_norm, 0.36))
    cosine, sine = sincos_cycles(THICKNESS * (axial_root - 1.0))
    scale = jnp.where(inside, 1.0 / float(N * N), 0.0)
    return scale * cosine, scale * sine


def kernel(
    tilts, index_ref, wide, narrow, col_twist, row_twist, out_ref,
    strip, incident, section, send_a, recv_a, send_b, recv_b, pupil,
    gather_send, gather_recv, a_send, a_recv, b_send, b_recv,
):
    group = lax.axis_index("group")
    me = lax.axis_index("rows")

    def table(ref, place):
        rows = pl.ds(place[0], place[1])
        return ref[0, rows, :], ref[1, rows, :]

    barrier = pltpu.get_barrier_semaphore()

    def greet_group(step, carry):
        peer = lax.rem(group + step, GROUPS)
        pl.semaphore_signal(barrier, inc=1, device_id={"group": peer}, device_id_type=MESH)
        return carry

    def greet_rows(step, carry):
        peer = lax.rem(me + step, ROWS)
        pl.semaphore_signal(barrier, inc=1, device_id={"rows": peer}, device_id_type=MESH)
        return carry

    lax.fori_loop(1, GROUPS, greet_group, 0)
    lax.fori_loop(1, ROWS, greet_rows, 0)
    pl.semaphore_wait(barrier, GROUPS - 1 + ROWS - 1)

    gathers = []
    for step in range(1, GROUPS):
        peer = lax.rem(group + step, GROUPS)
        copy = pltpu.make_async_remote_copy(
            src_ref=index_ref,
            dst_ref=strip.at[group],
            send_sem=gather_send.at[step],
            recv_sem=gather_recv.at[step],
            device_id={"group": peer},
            device_id_type=MESH,
        )
        copy.start()
        gathers.append(copy)
    strip[group] = index_ref[...]

    tilt_row, tilt_col = tilts[0, 0], tilts[0, 1]
    pos_row = me * STRIP + lax.broadcasted_iota(jnp.int32, (STRIP, HIGH), 0)
    pos_col = lax.broadcasted_iota(jnp.int32, (STRIP, HIGH), 1)
    base = tilt_row * pos_row + tilt_col * pos_col
    for y1 in range(LOW):
        residue = (base + tilt_col * (HIGH * y1)) & (N - 1)
        cosine, sine = sincos_cycles(residue.astype(jnp.float32) * (1.0 / N))
        incident[0, y1] = cosine
        incident[1, y1] = sine

    lane = lax.broadcasted_iota(jnp.int32, (ROWS, FOLD * STRIP), 1)
    natural = lax.broadcasted_iota(jnp.int32, (ROWS, FOLD * STRIP), 0) + ROWS * lax.rem(lane, STRIP)
    freq_rows = jnp.where(natural < N // 2, natural, natural - N)
    tile_me = me // SLOTS
    slot_me = lax.rem(me, SLOTS)
    freq_cols = tile_me * FOLD + lane // STRIP + LOW * (slot_me * SUB - BANDS // 2)
    for sub in range(SUB):
        real, imag = pupil_parts(freq_rows, freq_cols + LOW * sub)
        pupil[0, sub] = real
        pupil[1, sub] = imag

    for copy in gathers:
        copy.wait()

    for part in range(STRIP // 8):
        rows = pl.ds(8 * part, 8)
        values = []
        for y1 in range(LOW):
            lanes = pl.ds(HIGH * (y1 % 2), HIGH)
            contrast = strip[y1 // 2, rows, lanes]
            screen = sincos_small(contrast * (2.0 * math.pi * THICKNESS))
            values.append(cmul(screen, (incident[0, y1, rows, :], incident[1, y1, rows, :])))
        values = dft16(values, -1)
        for kap in range(LOW):
            twist = (col_twist[0, pl.ds(kap, 1), :], -col_twist[1, pl.ds(kap, 1), :])
            real, imag = cmul(values[kap], twist)
            place = pl.ds(kap * STRIP + 8 * part, 8)
            section[place, pl.ds(0, HIGH)] = real
            section[place, pl.ds(HIGH, HIGH)] = imag

    forward = table(wide, COL_FWD)
    for tile in range(TILES):
        data = split(section[pl.ds(tile * FOLD * STRIP, FOLD * STRIP), :])
        send_a[pl.ds(tile * 2 * BANDS, 2 * BANDS), :] = dot3(forward, data, ((1,), (1,)))

    def exchange(source, target, send_sem, recv_sem):
        def send_one(step, carry):
            peer = lax.rem(me + step, ROWS)
            pltpu.make_async_remote_copy(
                src_ref=source.at[pl.ds(peer * MSG, MSG), :],
                dst_ref=target.at[pl.ds(me * MSG, MSG), :],
                send_sem=send_sem,
                recv_sem=recv_sem,
                device_id={"rows": peer},
                device_id_type=MESH,
            ).start()
            return carry

        lax.fori_loop(1, ROWS, send_one, 0)
        target[pl.ds(me * MSG, MSG), :] = source[pl.ds(me * MSG, MSG), :]
        every = pl.ds(0, (ROWS - 1) * MSG)
        return pltpu.make_async_remote_copy(
            src_ref=source.at[every, :],
            dst_ref=target.at[every, :],
            send_sem=send_sem,
            recv_sem=recv_sem,
            device_id={"rows": lax.rem(me + 1, ROWS)},
            device_id_type=MESH,
        )

    first = exchange(send_a, recv_a, a_send, a_recv)
    first.wait_recv()

    parts = [
        jnp.concatenate(
            [recv_a[pl.ds(sub, ROWS, stride=MSG), :], recv_a[pl.ds(SUB + sub, ROWS, stride=MSG), :]], axis=0
        )
        for sub in range(SUB)
    ]
    lanes = FOLD * STRIP
    data = split(jnp.concatenate(parts, axis=1))
    data = dot3(table(narrow, ROW_FWD), data, ((1,), (0,)))
    twist_cos, twist_sin = row_twist[0], row_twist[1]
    parts = []
    for sub in range(SUB):
        real, imag = data[:ROWS, sub * lanes : (sub + 1) * lanes], data[ROWS:, sub * lanes : (sub + 1) * lanes]
        parts.append(jnp.concatenate(cmul((real, imag), (twist_cos, -twist_sin)), axis=1))
    data = dot3(split(jnp.concatenate(parts, axis=0)), table(wide, IN_FWD), ((1,), (0,)))
    parts = []
    for sub in range(SUB):
        rows = slice(sub * ROWS, (sub + 1) * ROWS)
        real, imag = data[rows, :lanes], data[rows, lanes:]
        parts.append(jnp.concatenate(cmul((real, imag), (pupil[0, sub], pupil[1, sub])), axis=1))
    data = dot3(split(jnp.concatenate(parts, axis=0)), table(wide, IN_INV), ((1,), (0,)))
    parts = []
    for sub in range(SUB):
        rows = slice(sub * ROWS, (sub + 1) * ROWS)
        real, imag = data[rows, :lanes], data[rows, lanes:]
        parts.append(jnp.concatenate(cmul((real, imag), (twist_cos, twist_sin)), axis=0))
    data = dot3(table(narrow, ROW_INV), split(jnp.concatenate(parts, axis=1)), ((1,), (0,)))
    for sub in range(SUB):
        columns = slice(sub * lanes, (sub + 1) * lanes)
        send_b[pl.ds(sub, ROWS, stride=MSG), :] = data[:ROWS, columns]
        send_b[pl.ds(SUB + sub, ROWS, stride=MSG), :] = data[ROWS:, columns]

    second = exchange(send_b, recv_b, b_send, b_recv)
    second.wait_recv()

    inverse = table(wide, COL_INV)
    for tile in range(TILES):
        data = split(recv_b[pl.ds(tile * 2 * BANDS, 2 * BANDS), :].T)
        section[pl.ds(tile * lanes, lanes), :] = dot3(data, inverse, ((1,), (0,)))
    for part in range(STRIP // 8):
        values = []
        for kap in range(LOW):
            place = pl.ds(kap * STRIP + 8 * part, 8)
            twist = (col_twist[0, pl.ds(kap, 1), :], col_twist[1, pl.ds(kap, 1), :])
            values.append(cmul((section[place, pl.ds(0, HIGH)], section[place, pl.ds(HIGH, HIGH)]), twist))
        values = dft16(values, 1)
        for y1 in range(LOW):
            for plane in range(2):
                out_ref[plane, pl.ds(8 * part, 8), pl.ds(HIGH * y1, HIGH)] = values[y1][plane]

    first.wait_send()
    second.wait_send()


def per_device(illum_tilts, index_layers, measured):
    wide, narrow, col_twist, row_twist = tables()
    vmem = pl.BlockSpec(memory_space=pltpu.VMEM)
    field = pl.pallas_call(
        kernel,
        out_shape=jax.ShapeDtypeStruct((2, STRIP, N), jnp.float32),
        in_specs=[pl.BlockSpec(memory_space=pltpu.SMEM)] + [vmem] * 5,
        out_specs=vmem,
        scratch_shapes=[
            pltpu.VMEM((GROUPS, STRIP, N // GROUPS), jnp.float32),
            pltpu.VMEM((2, LOW, STRIP, HIGH), jnp.float32),
            pltpu.VMEM((LOW * STRIP, 2 * HIGH), jnp.float32),
            pltpu.VMEM((ROWS * MSG, FOLD * STRIP), jnp.float32),
            pltpu.VMEM((ROWS * MSG, FOLD * STRIP), jnp.float32),
            pltpu.VMEM((ROWS * MSG, FOLD * STRIP), jnp.float32),
            pltpu.VMEM((ROWS * MSG, FOLD * STRIP), jnp.float32),
            pltpu.VMEM((2, SUB, ROWS, FOLD * STRIP), jnp.float32),
            pltpu.SemaphoreType.DMA((GROUPS,)),
            pltpu.SemaphoreType.DMA((GROUPS,)),
            pltpu.SemaphoreType.DMA,
            pltpu.SemaphoreType.DMA,
            pltpu.SemaphoreType.DMA,
            pltpu.SemaphoreType.DMA,
        ],
        compiler_params=pltpu.CompilerParams(
            collective_id=0, has_side_effects=True, vmem_limit_bytes=32 * 1024 * 1024
        ),
    )(
        illum_tilts,
        index_layers[0],
        jnp.asarray(wide),
        jnp.asarray(narrow),
        jnp.asarray(col_twist),
        jnp.asarray(row_twist),
    )
    return field[None] - measured


def solution(mesh):
    return jax.shard_map(
        per_device,
        mesh=mesh,
        in_specs=(P("group", None), P(None, "rows", "group"), P("group", None, "rows", None)),
        out_specs=P("group", None, "rows", None),
        check_vma=False,
    )
```

```python
import math

import jax
import jax.numpy as jnp
import ml_dtypes
import numpy as np
from jax import lax
from jax.experimental import pallas as pl
from jax.experimental.pallas import tpu as pltpu
from jax.sharding import PartitionSpec as P

N = 2048
THICKNESS = 4.0
MESH = pl.DeviceIdType.MESH

GROUPS = 8
ROWS = 64
STRIP = N // ROWS
LOW = 16
HIGH = 128
BANDS = 80
SUB = 5
FOLD = 4
MSG = 2 * SUB
TILES = LOW // FOLD
SLOTS = BANDS // SUB


def split_const(table):
    high = table.astype(ml_dtypes.bfloat16)
    low = (table - high.astype(np.float64)).astype(ml_dtypes.bfloat16)
    return high, low


def real_form(cosine, sine):
    return np.block([[cosine, -sine], [sine, cosine]])


def tables():
    two_pi = 2.0 * math.pi
    m = np.arange(BANDS) - BANDS // 2
    angle = two_pi * ((m[:, None] * np.arange(HIGH)[None, :]) % HIGH) / HIGH
    forward = real_form(np.cos(angle), -np.sin(angle)).reshape(2, SLOTS, SUB, 2 * HIGH)
    col_fwd = forward.transpose(1, 0, 2, 3).reshape(2 * BANDS, 2 * HIGH)
    inverse = real_form(np.cos(angle.T), np.sin(angle.T)).reshape(2 * HIGH, 2, SLOTS, SUB)
    col_inv = inverse.transpose(2, 1, 3, 0).reshape(2 * BANDS, 2 * HIGH)
    step = np.arange(ROWS)
    angle = two_pi * ((step[:, None] * step[None, :]) % ROWS) / ROWS
    row_fwd = real_form(np.cos(angle), -np.sin(angle))
    row_inv = real_form(np.cos(angle), np.sin(angle))
    step = np.arange(STRIP)
    angle = two_pi * ((step[:, None] * step[None, :]) % STRIP) / STRIP
    eye = np.eye(FOLD)
    cosine, sine = np.kron(eye, np.cos(angle)), np.kron(eye, np.sin(angle))
    in_fwd = real_form(cosine, -sine).T
    in_inv = real_form(cosine, sine).T
    angle = two_pi * (np.arange(LOW)[:, None] * np.arange(HIGH)[None, :]) / N
    col_twist = np.stack([np.cos(angle), np.sin(angle)]).astype(np.float32)
    angle = two_pi * (np.arange(ROWS)[:, None] * np.arange(STRIP)[None, :]) / N
    row_twist = np.stack([np.tile(np.cos(angle), FOLD), np.tile(np.sin(angle), FOLD)]).astype(
        np.float32
    )
    wide = np.stack(split_const(np.concatenate([col_fwd, col_inv, in_fwd, in_inv])))
    narrow = np.stack(split_const(np.concatenate([row_fwd, row_inv])))
    return wide, narrow, col_twist, row_twist


COL_FWD = (0, 2 * BANDS)
COL_INV = (2 * BANDS, 2 * BANDS)
IN_FWD = (4 * BANDS, 2 * HIGH)
IN_INV = (4 * BANDS + 2 * HIGH, 2 * HIGH)
ROW_FWD = (0, 2 * ROWS)
ROW_INV = (2 * ROWS, 2 * ROWS)


def sincos_cycles(cycles):
    cycles = cycles - jnp.round(cycles)
    quarter = cycles * (0.5 * math.pi)
    square = quarter * quarter
    sine = quarter * (
        1.0 + square * (-1.0 / 6 + square * (1.0 / 120 + square * (-1.0 / 5040 + square * (1.0 / 362880))))
    )
    cosine = 1.0 + square * (
        -0.5 + square * (1.0 / 24 + square * (-1.0 / 720 + square * (1.0 / 40320 - square * (1.0 / 3628800))))
    )
    sine, cosine = 2.0 * sine * cosine, 1.0 - 2.0 * sine * sine
    sine, cosine = 2.0 * sine * cosine, 1.0 - 2.0 * sine * sine
    return cosine, sine


def sincos_small(angle):
    square = angle * angle
    sine = angle * (1.0 + square * (-1.0 / 6 + square * (1.0 / 120 - square * (1.0 / 5040))))
    cosine = 1.0 + square * (-0.5 + square * (1.0 / 24 + square * (-1.0 / 720 + square * (1.0 / 40320))))
    return cosine, sine


def cmul(a, b):
    return (a[0] * b[0] - a[1] * b[1], a[0] * b[1] + a[1] * b[0])


def cadd(a, b):
    return (a[0] + b[0], a[1] + b[1])


def csub(a, b):
    return (a[0] - b[0], a[1] - b[1])


def dft4(a, sign):
    even, odd = cadd(a[0], a[2]), cadd(a[1], a[3])
    even_d, odd_d = csub(a[0], a[2]), csub(a[1], a[3])
    turned = (-odd_d[1], odd_d[0]) if sign > 0 else (odd_d[1], -odd_d[0])
    return [cadd(even, odd), cadd(even_d, turned), csub(even, odd), csub(even_d, turned)]


def dft16(v, sign):
    half = math.sqrt(0.5)
    firsts = [dft4([v[4 * n1 + n2] for n1 in range(4)], sign) for n2 in range(4)]
    out = [None] * 16
    for k1 in range(4):
        column = []
        for n2 in range(4):
            re, im = firsts[n2][k1]
            turn = n2 * k1
            if turn == 2:
                re, im = (
                    (half * (re - im), half * (re + im)) if sign > 0 else (half * (re + im), half * (im - re))
                )
            elif turn == 4:
                re, im = (-im, re) if sign > 0 else (im, -re)
            elif turn == 6:
                re, im = (
                    (-half * (re + im), half * (re - im)) if sign > 0 else (half * (im - re), -half * (re + im))
                )
            elif turn:
                angle = 2.0 * math.pi * turn / 16
                re, im = cmul((re, im), (math.cos(angle), sign * math.sin(angle)))
            column.append((re, im))
        for k2, value in enumerate(dft4(column, sign)):
            out[k1 + 4 * k2] = value
    return out


def split(value):
    high = value.astype(jnp.bfloat16)
    low = (value - high.astype(jnp.float32)).astype(jnp.bfloat16)
    return high, low


def dot3(a, b, dims):
    def one(x, y):
        return lax.dot_general(x, y, (dims, ((), ())), preferred_element_type=jnp.float32)

    return one(a[0], b[0]) + (one(a[0], b[1]) + one(a[1], b[0]))


def pupil_parts(freq_rows, freq_cols):
    radius = freq_rows * freq_rows + freq_cols * freq_cols
    inside = 100 * radius < 9 * N * N
    radius_norm = radius.astype(jnp.float32) * (1.0 / float((N // 2) ** 2))
    axial_root = jnp.sqrt(1.0 - jnp.minimum(radius_norm, 0.36))
    cosine, sine = sincos_cycles(THICKNESS * (axial_root - 1.0))
    scale = jnp.where(inside, 1.0 / float(N * N), 0.0)
    return scale * cosine, scale * sine


def kernel(
    tilts_hbm, index_ref, wide_hbm, narrow_hbm, col_hbm, row_hbm, out_ref,
    strip, incident, section, send_a, recv_a, send_b, recv_b, pupil,
    tilts, wide, narrow, col_twist, row_twist,
    gather_send, gather_recv, pass_send, pass_recv, plane_sem, pair_sem, a_send, a_recv, b_send, b_recv, load_sems,
):
    group = lax.axis_index("group")
    me = lax.axis_index("rows")
    loads = [
        pltpu.make_async_copy(source, target, load_sems.at[place])
        for place, (source, target) in enumerate(
            [
                (tilts_hbm, tilts),
                (index_ref, strip.at[group]),
                (col_hbm, col_twist),
                (wide_hbm, wide),
                (narrow_hbm, narrow),
                (row_hbm, row_twist),
            ]
        )
    ]
    for load in loads:
        load.start()

    def table(ref, place):
        rows = pl.ds(place[0], place[1])
        return ref[0, rows, :], ref[1, rows, :]

    side = lax.rem(group, 2)
    partner = group + 1 - 2 * side
    place_z, place_x, place_y = me // 32, lax.rem(me // 8, 4), lax.rem(me, 8)
    peers_y = [me - place_y + lax.rem(place_y + step, 8) for step in range(1, 8)]
    peers_x = [me + 8 * (lax.rem(place_x + step, 4) - place_x) for step in range(1, 4)]
    peer_z = me + 32 * (1 - 2 * place_z)
    peers_group = [lax.rem(group + 2 * step, GROUPS) for step in (2, 1, 3)]

    def signal(sem, axis, peer):
        pl.semaphore_signal(sem, inc=1, device_id={axis: peer}, device_id_type=MESH)

    with jax.named_scope("greet"):
        barrier = pltpu.get_barrier_semaphore()
        for peer in peers_group + [partner]:
            signal(barrier, "group", peer)
        for peer in peers_y + peers_x + [peer_z]:
            signal(barrier, "rows", peer)
        pl.semaphore_wait(barrier, 15)

    def piece(owner, sems, slot, peer):
        return pltpu.make_async_remote_copy(
            src_ref=strip.at[owner],
            dst_ref=strip.at[owner],
            send_sem=sems[0].at[slot],
            recv_sem=sems[1].at[slot],
            device_id={"group": peer},
            device_id_type=MESH,
        )

    gather_sems, pass_sems = (gather_send, gather_recv), (pass_send, pass_recv)
    with jax.named_scope("gather_start"):
        loads[1].wait()
        gathers = [piece(group, gather_sems, slot, peer) for slot, peer in enumerate(peers_group)]
        passes = [piece(group, pass_sems, 3, partner)]
        for copy in gathers + passes:
            copy.start()
    with jax.named_scope("report"):
        for peer in peers_x:
            signal(plane_sem, "rows", peer)
        pl.semaphore_wait(plane_sem, 3)
        signal(pair_sem, "rows", peer_z)
        pl.semaphore_wait(pair_sem, 1)

    with jax.named_scope("incident_pupil"):
        loads[0].wait()
        tilt_row, tilt_col = tilts[0, 0], tilts[0, 1]
        pos_row = me * STRIP + lax.broadcasted_iota(jnp.int32, (STRIP, HIGH), 0)
        pos_col = lax.broadcasted_iota(jnp.int32, (STRIP, HIGH), 1)
        base = tilt_row * pos_row + tilt_col * pos_col
        for y1 in range(LOW):
            residue = (base + tilt_col * (HIGH * y1)) & (N - 1)
            cosine, sine = sincos_cycles(residue.astype(jnp.float32) * (1.0 / N))
            incident[0, y1] = cosine
            incident[1, y1] = sine

        lane = lax.broadcasted_iota(jnp.int32, (ROWS, FOLD * STRIP), 1)
        natural = lax.broadcasted_iota(jnp.int32, (ROWS, FOLD * STRIP), 0) + ROWS * lax.rem(lane, STRIP)
        freq_rows = jnp.where(natural < N // 2, natural, natural - N)
        tile_me = me // SLOTS
        slot_me = lax.rem(me, SLOTS)
        freq_cols = tile_me * FOLD + lane // STRIP + LOW * (slot_me * SUB - BANDS // 2)
        for sub in range(SUB):
            real, imag = pupil_parts(freq_rows, freq_cols + LOW * sub)
            pupil[0, sub] = real
            pupil[1, sub] = imag

    with jax.named_scope("gather_wait"):
        for slot, step in ((1, 3), (2, 1), (0, 2)):
            gathers[slot].wait_recv()
            copy = piece(lax.rem(group + 2 * step, GROUPS), pass_sems, slot, partner)
            copy.start()
            passes.append(copy)
        for copy in passes:
            copy.wait()
        for copy in gathers:
            copy.wait_send()
        for place in (2, 3, 4, 5):
            loads[place].wait()

    with jax.named_scope("screen_dft16"):
        for part in range(STRIP // 8):
            rows = pl.ds(8 * part, 8)
            values = []
            for y1 in range(LOW):
                lanes = pl.ds(HIGH * (y1 % 2), HIGH)
                contrast = strip[y1 // 2, rows, lanes]
                screen = sincos_small(contrast * (2.0 * math.pi * THICKNESS))
                values.append(cmul(screen, (incident[0, y1, rows, :], incident[1, y1, rows, :])))
            values = dft16(values, -1)
            for kap in range(LOW):
                twist = (col_twist[0, pl.ds(kap, 1), :], -col_twist[1, pl.ds(kap, 1), :])
                real, imag = cmul(values[kap], twist)
                place = pl.ds(kap * STRIP + 8 * part, 8)
                section[place, pl.ds(0, HIGH)] = real
                section[place, pl.ds(HIGH, HIGH)] = imag

    with jax.named_scope("column_128"):
        forward = table(wide, COL_FWD)
        for tile in range(TILES):
            data = split(section[pl.ds(tile * FOLD * STRIP, FOLD * STRIP), :])
            send_a[pl.ds(tile * 2 * BANDS, 2 * BANDS), :] = dot3(forward, data, ((1,), (1,)))

    def exchange(source, target, send_sem, recv_sem):
        def far_first(step, size):
            return lax.rem(size // 2 + size + (1 - 2 * lax.rem(step, 2)) * ((step + 1) // 2), size)

        def send_one(step, carry):
            to_y = lax.rem(place_y + far_first(step // 8, 8), 8)
            to_x = lax.rem(place_x + far_first(lax.rem(step // 2, 4), 4), 4)
            to_z = lax.rem(place_z + 1 + lax.rem(step, 2), 2)
            peer = to_z * 32 + to_x * 8 + to_y
            pltpu.make_async_remote_copy(
                src_ref=source.at[pl.ds(peer * MSG, MSG), :],
                dst_ref=target.at[pl.ds(me * MSG, MSG), :],
                send_sem=send_sem,
                recv_sem=recv_sem,
                device_id={"rows": peer},
                device_id_type=MESH,
            ).start()
            return carry

        lax.fori_loop(0, ROWS - 1, send_one, 0)
        target[pl.ds(me * MSG, MSG), :] = source[pl.ds(me * MSG, MSG), :]
        every = pl.ds(0, (ROWS - 1) * MSG)
        return pltpu.make_async_remote_copy(
            src_ref=source.at[every, :],
            dst_ref=target.at[every, :],
            send_sem=send_sem,
            recv_sem=recv_sem,
            device_id={"rows": lax.rem(me + 1, ROWS)},
            device_id_type=MESH,
        )

    with jax.named_scope("exchange_a_start"):
        first = exchange(send_a, recv_a, a_send, a_recv)
    with jax.named_scope("exchange_a_wait"):
        first.wait_recv()

    with jax.named_scope("row_work"):
        parts = [
            jnp.concatenate(
                [recv_a[pl.ds(sub, ROWS, stride=MSG), :], recv_a[pl.ds(SUB + sub, ROWS, stride=MSG), :]], axis=0
            )
            for sub in range(SUB)
        ]
        lanes = FOLD * STRIP
        data = split(jnp.concatenate(parts, axis=1))
        data = dot3(table(narrow, ROW_FWD), data, ((1,), (0,)))
        twist_cos, twist_sin = row_twist[0], row_twist[1]
        parts = []
        for sub in range(SUB):
            real, imag = data[:ROWS, sub * lanes : (sub + 1) * lanes], data[ROWS:, sub * lanes : (sub + 1) * lanes]
            parts.append(jnp.concatenate(cmul((real, imag), (twist_cos, -twist_sin)), axis=1))
        data = dot3(split(jnp.concatenate(parts, axis=0)), table(wide, IN_FWD), ((1,), (0,)))
        parts = []
        for sub in range(SUB):
            rows = slice(sub * ROWS, (sub + 1) * ROWS)
            real, imag = data[rows, :lanes], data[rows, lanes:]
            parts.append(jnp.concatenate(cmul((real, imag), (pupil[0, sub], pupil[1, sub])), axis=1))
        data = dot3(split(jnp.concatenate(parts, axis=0)), table(wide, IN_INV), ((1,), (0,)))
        parts = []
        for sub in range(SUB):
            rows = slice(sub * ROWS, (sub + 1) * ROWS)
            real, imag = data[rows, :lanes], data[rows, lanes:]
            parts.append(jnp.concatenate(cmul((real, imag), (twist_cos, twist_sin)), axis=0))
        data = dot3(table(narrow, ROW_INV), split(jnp.concatenate(parts, axis=1)), ((1,), (0,)))
        for sub in range(SUB):
            columns = slice(sub * lanes, (sub + 1) * lanes)
            send_b[pl.ds(sub, ROWS, stride=MSG), :] = data[:ROWS, columns]
            send_b[pl.ds(SUB + sub, ROWS, stride=MSG), :] = data[ROWS:, columns]

    with jax.named_scope("exchange_b_start"):
        second = exchange(send_b, recv_b, b_send, b_recv)
    with jax.named_scope("exchange_b_wait"):
        second.wait_recv()

    with jax.named_scope("columns_back"):
        inverse = table(wide, COL_INV)
        for tile in range(TILES):
            data = split(recv_b[pl.ds(tile * 2 * BANDS, 2 * BANDS), :].T)
            section[pl.ds(tile * lanes, lanes), :] = dot3(data, inverse, ((1,), (0,)))
        for part in range(STRIP // 8):
            values = []
            for kap in range(LOW):
                place = pl.ds(kap * STRIP + 8 * part, 8)
                twist = (col_twist[0, pl.ds(kap, 1), :], col_twist[1, pl.ds(kap, 1), :])
                values.append(cmul((section[place, pl.ds(0, HIGH)], section[place, pl.ds(HIGH, HIGH)]), twist))
            values = dft16(values, 1)
            for y1 in range(LOW):
                for plane in range(2):
                    out_ref[plane, pl.ds(8 * part, 8), pl.ds(HIGH * y1, HIGH)] = values[y1][plane]

    first.wait_send()
    second.wait_send()


def per_device(illum_tilts, index_layers, measured):
    wide, narrow, col_twist, row_twist = tables()
    vmem = pl.BlockSpec(memory_space=pltpu.VMEM)
    field = pl.pallas_call(
        kernel,
        out_shape=jax.ShapeDtypeStruct((2, STRIP, N), jnp.float32),
        in_specs=[pl.BlockSpec(memory_space=pltpu.HBM)] * 6,
        out_specs=vmem,
        scratch_shapes=[
            pltpu.VMEM((GROUPS, STRIP, N // GROUPS), jnp.float32),
            pltpu.VMEM((2, LOW, STRIP, HIGH), jnp.float32),
            pltpu.VMEM((LOW * STRIP, 2 * HIGH), jnp.float32),
            pltpu.VMEM((ROWS * MSG, FOLD * STRIP), jnp.float32),
            pltpu.VMEM((ROWS * MSG, FOLD * STRIP), jnp.float32),
            pltpu.VMEM((ROWS * MSG, FOLD * STRIP), jnp.float32),
            pltpu.VMEM((ROWS * MSG, FOLD * STRIP), jnp.float32),
            pltpu.VMEM((2, SUB, ROWS, FOLD * STRIP), jnp.float32),
            pltpu.SMEM((1, 2), jnp.int32),
            pltpu.VMEM(wide.shape, jnp.bfloat16),
            pltpu.VMEM(narrow.shape, jnp.bfloat16),
            pltpu.VMEM(col_twist.shape, jnp.float32),
            pltpu.VMEM(row_twist.shape, jnp.float32),
            pltpu.SemaphoreType.DMA((3,)),
            pltpu.SemaphoreType.DMA((3,)),
            pltpu.SemaphoreType.DMA((4,)),
            pltpu.SemaphoreType.DMA((4,)),
            pltpu.SemaphoreType.REGULAR,
            pltpu.SemaphoreType.REGULAR,
            pltpu.SemaphoreType.DMA,
            pltpu.SemaphoreType.DMA,
            pltpu.SemaphoreType.DMA,
            pltpu.SemaphoreType.DMA,
            pltpu.SemaphoreType.DMA((6,)),
        ],
        compiler_params=pltpu.CompilerParams(
            collective_id=0, has_side_effects=True, vmem_limit_bytes=60 * 1024 * 1024
        ),
    )(
        illum_tilts,
        index_layers[0],
        jnp.asarray(wide),
        jnp.asarray(narrow),
        jnp.asarray(col_twist),
        jnp.asarray(row_twist),
    )
    return field[None] - measured


def solution(mesh):
    return jax.shard_map(
        per_device,
        mesh=mesh,
        in_specs=(P("group", None), P(None, "rows", "group"), P("group", None, "rows", None)),
        out_specs=P("group", None, "rows", None),
        check_vma=False,
    )
```

```python
import math

import jax
import jax.numpy as jnp
import ml_dtypes
import numpy as np
from jax import lax
from jax.experimental import pallas as pl
from jax.experimental.pallas import tpu as pltpu
from jax.sharding import PartitionSpec as P

N = 2048
THICKNESS = 4.0
MESH = pl.DeviceIdType.MESH

GROUPS = 8
ROWS = 64
STRIP = N // ROWS
LOW = 16
HIGH = 128
BANDS = 80
SUB = 5
FOLD = 4
CHUNKS = ((0, 2), (2, 4), (4, 5))
TILES = LOW // FOLD
SLOTS = BANDS // SUB


def split_const(table):
    high = table.astype(ml_dtypes.bfloat16)
    low = (table - high.astype(np.float64)).astype(ml_dtypes.bfloat16)
    return high, low


def real_form(cosine, sine):
    return np.block([[cosine, -sine], [sine, cosine]])


def tables():
    two_pi = 2.0 * math.pi
    m = np.arange(BANDS) - BANDS // 2
    angle = two_pi * ((m[:, None] * np.arange(HIGH)[None, :]) % HIGH) / HIGH
    forward = real_form(np.cos(angle), -np.sin(angle)).reshape(2, SLOTS, SUB, 2 * HIGH)
    forward = forward.transpose(1, 0, 2, 3)
    inverse = real_form(np.cos(angle.T), np.sin(angle.T)).reshape(2 * HIGH, 2, SLOTS, SUB)
    inverse = inverse.transpose(2, 1, 3, 0)
    col_fwd, col_inv = (
        np.concatenate([table[:, :, lo:hi].reshape(-1, 2 * HIGH) for lo, hi in CHUNKS])
        for table in (forward, inverse)
    )
    step = np.arange(ROWS)
    angle = two_pi * ((step[:, None] * step[None, :]) % ROWS) / ROWS
    row_fwd = real_form(np.cos(angle), -np.sin(angle))
    row_inv = real_form(np.cos(angle), np.sin(angle))
    step = np.arange(STRIP)
    angle = two_pi * ((step[:, None] * step[None, :]) % STRIP) / STRIP
    eye = np.eye(FOLD)
    cosine, sine = np.kron(eye, np.cos(angle)), np.kron(eye, np.sin(angle))
    in_fwd = real_form(cosine, -sine).T
    in_inv = real_form(cosine, sine).T
    angle = two_pi * (np.arange(LOW)[:, None] * np.arange(HIGH)[None, :]) / N
    col_twist = np.stack([np.cos(angle), np.sin(angle)]).astype(np.float32)
    angle = two_pi * (np.arange(ROWS)[:, None] * np.arange(STRIP)[None, :]) / N
    row_twist = np.stack([np.tile(np.cos(angle), FOLD), np.tile(np.sin(angle), FOLD)]).astype(
        np.float32
    )
    wide = np.stack(split_const(np.concatenate([col_fwd, col_inv, in_fwd, in_inv])))
    narrow = np.stack(split_const(np.concatenate([row_fwd, row_inv])))
    return wide, narrow, col_twist, row_twist


CHUNK_ROWS = [(2 * SLOTS * lo, 2 * SLOTS * (hi - lo)) for lo, hi in CHUNKS]
COL_FWD = (0, 2 * BANDS)
COL_INV = (2 * BANDS, 2 * BANDS)
IN_FWD = (4 * BANDS, 2 * HIGH)
IN_INV = (4 * BANDS + 2 * HIGH, 2 * HIGH)
ROW_FWD = (0, 2 * ROWS)
ROW_INV = (2 * ROWS, 2 * ROWS)


def sincos_cycles(cycles):
    cycles = cycles - jnp.round(cycles)
    quarter = cycles * (0.5 * math.pi)
    square = quarter * quarter
    sine = quarter * (
        1.0 + square * (-1.0 / 6 + square * (1.0 / 120 + square * (-1.0 / 5040 + square * (1.0 / 362880))))
    )
    cosine = 1.0 + square * (
        -0.5 + square * (1.0 / 24 + square * (-1.0 / 720 + square * (1.0 / 40320 - square * (1.0 / 3628800))))
    )
    sine, cosine = 2.0 * sine * cosine, 1.0 - 2.0 * sine * sine
    sine, cosine = 2.0 * sine * cosine, 1.0 - 2.0 * sine * sine
    return cosine, sine


def sincos_small(angle):
    square = angle * angle
    sine = angle * (1.0 + square * (-1.0 / 6 + square * (1.0 / 120 - square * (1.0 / 5040))))
    cosine = 1.0 + square * (-0.5 + square * (1.0 / 24 + square * (-1.0 / 720 + square * (1.0 / 40320))))
    return cosine, sine


def cmul(a, b):
    return (a[0] * b[0] - a[1] * b[1], a[0] * b[1] + a[1] * b[0])


def cadd(a, b):
    return (a[0] + b[0], a[1] + b[1])


def csub(a, b):
    return (a[0] - b[0], a[1] - b[1])


def dft4(a, sign):
    even, odd = cadd(a[0], a[2]), cadd(a[1], a[3])
    even_d, odd_d = csub(a[0], a[2]), csub(a[1], a[3])
    turned = (-odd_d[1], odd_d[0]) if sign > 0 else (odd_d[1], -odd_d[0])
    return [cadd(even, odd), cadd(even_d, turned), csub(even, odd), csub(even_d, turned)]


def dft16(v, sign):
    half = math.sqrt(0.5)
    firsts = [dft4([v[4 * n1 + n2] for n1 in range(4)], sign) for n2 in range(4)]
    out = [None] * 16
    for k1 in range(4):
        column = []
        for n2 in range(4):
            re, im = firsts[n2][k1]
            turn = n2 * k1
            if turn == 2:
                re, im = (
                    (half * (re - im), half * (re + im)) if sign > 0 else (half * (re + im), half * (im - re))
                )
            elif turn == 4:
                re, im = (-im, re) if sign > 0 else (im, -re)
            elif turn == 6:
                re, im = (
                    (-half * (re + im), half * (re - im)) if sign > 0 else (half * (im - re), -half * (re + im))
                )
            elif turn:
                angle = 2.0 * math.pi * turn / 16
                re, im = cmul((re, im), (math.cos(angle), sign * math.sin(angle)))
            column.append((re, im))
        for k2, value in enumerate(dft4(column, sign)):
            out[k1 + 4 * k2] = value
    return out


def split(value):
    high = value.astype(jnp.bfloat16)
    low = (value - high.astype(jnp.float32)).astype(jnp.bfloat16)
    return high, low


def dot3(a, b, dims):
    def one(x, y):
        return lax.dot_general(x, y, (dims, ((), ())), preferred_element_type=jnp.float32)

    return one(a[0], b[0]) + (one(a[0], b[1]) + one(a[1], b[0]))


def pupil_parts(freq_rows, freq_cols):
    radius = freq_rows * freq_rows + freq_cols * freq_cols
    inside = 100 * radius < 9 * N * N
    radius_norm = radius.astype(jnp.float32) * (1.0 / float((N // 2) ** 2))
    axial_root = jnp.sqrt(1.0 - jnp.minimum(radius_norm, 0.36))
    cosine, sine = sincos_cycles(THICKNESS * (axial_root - 1.0))
    scale = jnp.where(inside, 1.0 / float(N * N), 0.0)
    return scale * cosine, scale * sine


def kernel(
    tilts_hbm, index_ref, wide_hbm, narrow_hbm, col_hbm, row_hbm, out_ref,
    strip, incident, section, send_a, recv_a, send_b, recv_b, pupil,
    tilts, wide, narrow, col_twist, row_twist,
    gather_send, gather_recv, pass_send, pass_recv, plane_sem, pair_sem, a_send, a_recv, b_send, b_recv, load_sems,
):
    group = lax.axis_index("group")
    me = lax.axis_index("rows")
    loads = [
        pltpu.make_async_copy(source, target, load_sems.at[place])
        for place, (source, target) in enumerate(
            [
                (tilts_hbm, tilts),
                (index_ref, strip.at[group]),
                (col_hbm, col_twist),
                (wide_hbm, wide),
                (narrow_hbm, narrow),
                (row_hbm, row_twist),
            ]
        )
    ]
    for load in loads:
        load.start()

    def table(ref, place):
        rows = pl.ds(place[0], place[1])
        return ref[0, rows, :], ref[1, rows, :]

    side = lax.rem(group, 2)
    partner = group + 1 - 2 * side
    place_z, place_x, place_y = me // 32, lax.rem(me // 8, 4), lax.rem(me, 8)
    peers_y = [me - place_y + lax.rem(place_y + step, 8) for step in range(1, 8)]
    peers_x = [me + 8 * (lax.rem(place_x + step, 4) - place_x) for step in range(1, 4)]
    peer_z = me + 32 * (1 - 2 * place_z)
    peers_group = [lax.rem(group + 2 * step, GROUPS) for step in (2, 1, 3)]

    def signal(sem, axis, peer):
        pl.semaphore_signal(sem, inc=1, device_id={axis: peer}, device_id_type=MESH)

    with jax.named_scope("greet"):
        barrier = pltpu.get_barrier_semaphore()
        for peer in peers_group + [partner]:
            signal(barrier, "group", peer)
        for peer in peers_y + peers_x + [peer_z]:
            signal(barrier, "rows", peer)
        pl.semaphore_wait(barrier, 15)

    def piece(owner, sems, slot, peer):
        return pltpu.make_async_remote_copy(
            src_ref=strip.at[owner],
            dst_ref=strip.at[owner],
            send_sem=sems[0].at[slot],
            recv_sem=sems[1].at[slot],
            device_id={"group": peer},
            device_id_type=MESH,
        )

    gather_sems, pass_sems = (gather_send, gather_recv), (pass_send, pass_recv)
    with jax.named_scope("gather_start"):
        loads[1].wait()
        gathers = [piece(group, gather_sems, slot, peer) for slot, peer in enumerate(peers_group)]
        passes = [piece(group, pass_sems, 3, partner)]
        for copy in gathers + passes:
            copy.start()
    with jax.named_scope("report"):
        for peer in peers_x:
            signal(plane_sem, "rows", peer)
        pl.semaphore_wait(plane_sem, 3)
        signal(pair_sem, "rows", peer_z)
        pl.semaphore_wait(pair_sem, 1)

    with jax.named_scope("incident_pupil"):
        loads[0].wait()
        tilt_row, tilt_col = tilts[0, 0], tilts[0, 1]
        pos_row = me * STRIP + lax.broadcasted_iota(jnp.int32, (STRIP, HIGH), 0)
        pos_col = lax.broadcasted_iota(jnp.int32, (STRIP, HIGH), 1)
        base = tilt_row * pos_row + tilt_col * pos_col
        for y1 in range(LOW):
            residue = (base + tilt_col * (HIGH * y1)) & (N - 1)
            cosine, sine = sincos_cycles(residue.astype(jnp.float32) * (1.0 / N))
            incident[0, y1] = cosine
            incident[1, y1] = sine

        lane = lax.broadcasted_iota(jnp.int32, (ROWS, FOLD * STRIP), 1)
        natural = lax.broadcasted_iota(jnp.int32, (ROWS, FOLD * STRIP), 0) + ROWS * lax.rem(lane, STRIP)
        freq_rows = jnp.where(natural < N // 2, natural, natural - N)
        tile_me = me // SLOTS
        slot_me = lax.rem(me, SLOTS)
        freq_cols = tile_me * FOLD + lane // STRIP + LOW * (slot_me * SUB - BANDS // 2)
        for sub in range(SUB):
            real, imag = pupil_parts(freq_rows, freq_cols + LOW * sub)
            pupil[0, sub] = real
            pupil[1, sub] = imag

    with jax.named_scope("gather_wait"):
        for slot, step in ((1, 3), (2, 1), (0, 2)):
            gathers[slot].wait_recv()
            copy = piece(lax.rem(group + 2 * step, GROUPS), pass_sems, slot, partner)
            copy.start()
            passes.append(copy)
        for copy in passes:
            copy.wait()
        for copy in gathers:
            copy.wait_send()
        for place in (2, 3, 4, 5):
            loads[place].wait()

    with jax.named_scope("screen_dft16"):
        for part in range(STRIP // 8):
            rows = pl.ds(8 * part, 8)
            values = []
            for y1 in range(LOW):
                lanes = pl.ds(HIGH * (y1 % 2), HIGH)
                contrast = strip[y1 // 2, rows, lanes]
                screen = sincos_small(contrast * (2.0 * math.pi * THICKNESS))
                values.append(cmul(screen, (incident[0, y1, rows, :], incident[1, y1, rows, :])))
            values = dft16(values, -1)
            for kap in range(LOW):
                twist = (col_twist[0, pl.ds(kap, 1), :], -col_twist[1, pl.ds(kap, 1), :])
                real, imag = cmul(values[kap], twist)
                place = pl.ds(kap * STRIP + 8 * part, 8)
                section[place, pl.ds(0, HIGH)] = real
                section[place, pl.ds(HIGH, HIGH)] = imag

    with jax.named_scope("column_128"):
        lanes = FOLD * STRIP
        tiles = [split(section[pl.ds(tile * lanes, lanes), :]) for tile in range(TILES)]

    rows_y = {step: lax.rem(place_y + step, 8) for step in (4, 3, 5, 2, 6, 1, 7, 0)}
    rows_x = {step: 8 * lax.rem(place_x + step, 4) for step in (2, 1, 3, 0)}
    rows_z = {1: 32 * (1 - place_z), 0: 32 * place_z}
    peers = [rows_y[y] + (rows_x[x] + rows_z[z]) for y in rows_y for x in rows_x for z in rows_z if x or y or z]

    def exchange(source, target, send_sem, recv_sem):
        msg = source.shape[0] // ROWS
        here = pl.ds(me * msg, msg)
        for peer in peers:
            pltpu.make_async_remote_copy(
                src_ref=source.at[pl.ds(peer * msg, msg), :],
                dst_ref=target.at[here, :],
                send_sem=send_sem,
                recv_sem=recv_sem,
                device_id={"rows": peer},
                device_id_type=MESH,
            ).start()
        target[pl.ds(me * msg, msg), :] = source[pl.ds(me * msg, msg), :]
        every = pl.ds(0, (ROWS - 1) * msg)
        return pltpu.make_async_remote_copy(
            src_ref=source.at[every, :],
            dst_ref=target.at[every, :],
            send_sem=send_sem,
            recv_sem=recv_sem,
            device_id={"rows": peer_z},
            device_id_type=MESH,
        )

    exchanges = []
    for chunk, (start, size) in enumerate(CHUNK_ROWS):
        with jax.named_scope("column_exchange"):
            forward = table(wide, (COL_FWD[0] + start, size))
            for tile in range(TILES):
                send_a[chunk][pl.ds(tile * size, size), :] = dot3(forward, tiles[tile], ((1,), (1,)))
            exchanges.append(exchange(send_a[chunk], recv_a[chunk], a_send.at[chunk], a_recv.at[chunk]))

    twist_cos, twist_sin = row_twist[0], row_twist[1]
    for chunk, (first, last) in enumerate(CHUNKS):
        subs = last - first
        msg = 2 * subs
        with jax.named_scope("row_wait"):
            exchanges[chunk].wait_recv()
        with jax.named_scope("row_work"):
            got = recv_a[chunk]
            parts = [
                jnp.concatenate([got[pl.ds(part * subs + sub, ROWS, stride=msg), :] for part in range(2)], axis=0)
                for sub in range(subs)
            ]
            data = split(jnp.concatenate(parts, axis=1))
            data = dot3(table(narrow, ROW_FWD), data, ((1,), (0,)))
            parts = []
            for sub in range(subs):
                columns = slice(sub * lanes, (sub + 1) * lanes)
                value = cmul((data[:ROWS, columns], data[ROWS:, columns]), (twist_cos, -twist_sin))
                parts.append(jnp.concatenate(value, axis=1))
            data = dot3(split(jnp.concatenate(parts, axis=0)), table(wide, IN_FWD), ((1,), (0,)))
            parts = []
            for sub in range(subs):
                rows = slice(sub * ROWS, (sub + 1) * ROWS)
                mask = (pupil[0, first + sub], pupil[1, first + sub])
                parts.append(jnp.concatenate(cmul((data[rows, :lanes], data[rows, lanes:]), mask), axis=1))
            data = dot3(split(jnp.concatenate(parts, axis=0)), table(wide, IN_INV), ((1,), (0,)))
            parts = []
            for sub in range(subs):
                rows = slice(sub * ROWS, (sub + 1) * ROWS)
                value = cmul((data[rows, :lanes], data[rows, lanes:]), (twist_cos, twist_sin))
                parts.append(jnp.concatenate(value, axis=0))
            data = dot3(table(narrow, ROW_INV), split(jnp.concatenate(parts, axis=1)), ((1,), (0,)))
            for sub in range(subs):
                columns = slice(sub * lanes, (sub + 1) * lanes)
                for part in range(2):
                    place = pl.ds(part * subs + sub, ROWS, stride=msg)
                    send_b[chunk][place, :] = data[part * ROWS : (part + 1) * ROWS, columns]
        with jax.named_scope("row_exchange"):
            exchanges.append(exchange(send_b[chunk], recv_b[chunk], b_send.at[chunk], b_recv.at[chunk]))

    for chunk, (start, size) in enumerate(CHUNK_ROWS):
        with jax.named_scope("column_wait"):
            exchanges[len(CHUNKS) + chunk].wait_recv()
        with jax.named_scope("columns_back"):
            inverse = table(wide, (COL_INV[0] + start, size))
            for tile in range(TILES):
                data = split(recv_b[chunk][pl.ds(tile * size, size), :].T)
                value = dot3(data, inverse, ((1,), (0,)))
                place = pl.ds(tile * lanes, lanes)
                section[place, :] = value if chunk == 0 else section[place, :] + value
    with jax.named_scope("columns_last"):
        for part in range(STRIP // 8):
            values = []
            for kap in range(LOW):
                place = pl.ds(kap * STRIP + 8 * part, 8)
                twist = (col_twist[0, pl.ds(kap, 1), :], col_twist[1, pl.ds(kap, 1), :])
                values.append(cmul((section[place, pl.ds(0, HIGH)], section[place, pl.ds(HIGH, HIGH)]), twist))
            values = dft16(values, 1)
            for y1 in range(LOW):
                for plane in range(2):
                    out_ref[plane, pl.ds(8 * part, 8), pl.ds(HIGH * y1, HIGH)] = values[y1][plane]

    for copy in exchanges:
        copy.wait_send()


def per_device(illum_tilts, index_layers, measured):
    wide, narrow, col_twist, row_twist = tables()
    vmem = pl.BlockSpec(memory_space=pltpu.VMEM)
    messages = [pltpu.VMEM((2 * (hi - lo) * ROWS, FOLD * STRIP), jnp.float32) for lo, hi in CHUNKS]
    field = pl.pallas_call(
        kernel,
        out_shape=jax.ShapeDtypeStruct((2, STRIP, N), jnp.float32),
        in_specs=[pl.BlockSpec(memory_space=pltpu.HBM)] * 6,
        out_specs=vmem,
        scratch_shapes=[
            pltpu.VMEM((GROUPS, STRIP, N // GROUPS), jnp.float32),
            pltpu.VMEM((2, LOW, STRIP, HIGH), jnp.float32),
            pltpu.VMEM((LOW * STRIP, 2 * HIGH), jnp.float32),
            messages,
            messages,
            messages,
            messages,
            pltpu.VMEM((2, SUB, ROWS, FOLD * STRIP), jnp.float32),
            pltpu.SMEM((1, 2), jnp.int32),
            pltpu.VMEM(wide.shape, jnp.bfloat16),
            pltpu.VMEM(narrow.shape, jnp.bfloat16),
            pltpu.VMEM(col_twist.shape, jnp.float32),
            pltpu.VMEM(row_twist.shape, jnp.float32),
            pltpu.SemaphoreType.DMA((3,)),
            pltpu.SemaphoreType.DMA((3,)),
            pltpu.SemaphoreType.DMA((4,)),
            pltpu.SemaphoreType.DMA((4,)),
            pltpu.SemaphoreType.REGULAR,
            pltpu.SemaphoreType.REGULAR,
            pltpu.SemaphoreType.DMA((len(CHUNKS),)),
            pltpu.SemaphoreType.DMA((len(CHUNKS),)),
            pltpu.SemaphoreType.DMA((len(CHUNKS),)),
            pltpu.SemaphoreType.DMA((len(CHUNKS),)),
            pltpu.SemaphoreType.DMA((6,)),
        ],
        compiler_params=pltpu.CompilerParams(
            collective_id=0, has_side_effects=True, vmem_limit_bytes=60 * 1024 * 1024
        ),
    )(
        illum_tilts,
        index_layers[0],
        jnp.asarray(wide),
        jnp.asarray(narrow),
        jnp.asarray(col_twist),
        jnp.asarray(row_twist),
    )
    return field[None] - measured


def solution(mesh):
    return jax.shard_map(
        per_device,
        mesh=mesh,
        in_specs=(P("group", None), P(None, "rows", "group"), P("group", None, "rows", None)),
        out_specs=P("group", None, "rows", None),
        check_vma=False,
    )
```

```python
import math

import jax
import jax.numpy as jnp
import ml_dtypes
import numpy as np
from jax import lax
from jax.experimental import pallas as pl
from jax.experimental.pallas import tpu as pltpu
from jax.sharding import PartitionSpec as P

N = 2048
THICKNESS = 4.0
MESH = pl.DeviceIdType.MESH

GROUPS = 8
ROWS = 64
STRIP = N // ROWS
LOW = 16
HIGH = 128
BANDS = 80
SUB = 5
FOLD = 4
CHUNKS = ((0, 1), (1, 2), (2, 3), (3, 5))
TILES = LOW // FOLD
SLOTS = BANDS // SUB


def split_const(table):
    high = table.astype(ml_dtypes.bfloat16)
    low = (table - high.astype(np.float64)).astype(ml_dtypes.bfloat16)
    return high, low


def real_form(cosine, sine):
    return np.block([[cosine, -sine], [sine, cosine]])


def tables():
    two_pi = 2.0 * math.pi
    m = np.arange(BANDS) - BANDS // 2
    angle = two_pi * ((m[:, None] * np.arange(HIGH)[None, :]) % HIGH) / HIGH
    forward = real_form(np.cos(angle), -np.sin(angle)).reshape(2, SLOTS, SUB, 2 * HIGH)
    forward = forward.transpose(1, 0, 2, 3)
    inverse = real_form(np.cos(angle.T), np.sin(angle.T)).reshape(2 * HIGH, 2, SLOTS, SUB)
    inverse = inverse.transpose(2, 1, 3, 0)
    col_fwd, col_inv = (
        np.concatenate([table[:, :, lo:hi].reshape(-1, 2 * HIGH) for lo, hi in CHUNKS])
        for table in (forward, inverse)
    )
    step = np.arange(ROWS)
    angle = two_pi * ((step[:, None] * step[None, :]) % ROWS) / ROWS
    row_fwd = real_form(np.cos(angle), -np.sin(angle))
    row_inv = real_form(np.cos(angle), np.sin(angle))
    step = np.arange(STRIP)
    angle = two_pi * ((step[:, None] * step[None, :]) % STRIP) / STRIP
    eye = np.eye(FOLD)
    cosine, sine = np.kron(eye, np.cos(angle)), np.kron(eye, np.sin(angle))
    in_fwd = real_form(cosine, -sine).T
    in_inv = real_form(cosine, sine).T
    angle = two_pi * (np.arange(LOW)[:, None] * np.arange(HIGH)[None, :]) / N
    col_twist = np.stack([np.cos(angle), np.sin(angle)]).astype(np.float32)
    angle = two_pi * (np.arange(ROWS)[:, None] * np.arange(STRIP)[None, :]) / N
    row_twist = np.stack([np.tile(np.cos(angle), FOLD), np.tile(np.sin(angle), FOLD)]).astype(
        np.float32
    )
    wide = np.stack(split_const(np.concatenate([col_fwd, col_inv, in_fwd, in_inv])))
    narrow = np.stack(split_const(np.concatenate([row_fwd, row_inv])))
    return wide, narrow, col_twist, row_twist


CHUNK_ROWS = [(2 * SLOTS * lo, 2 * SLOTS * (hi - lo)) for lo, hi in CHUNKS]
COL_FWD = (0, 2 * BANDS)
COL_INV = (2 * BANDS, 2 * BANDS)
IN_FWD = (4 * BANDS, 2 * HIGH)
IN_INV = (4 * BANDS + 2 * HIGH, 2 * HIGH)
ROW_FWD = (0, 2 * ROWS)
ROW_INV = (2 * ROWS, 2 * ROWS)


def sincos_cycles(cycles):
    cycles = cycles - jnp.round(cycles)
    quarter = cycles * (0.5 * math.pi)
    square = quarter * quarter
    sine = quarter * (
        1.0 + square * (-1.0 / 6 + square * (1.0 / 120 + square * (-1.0 / 5040 + square * (1.0 / 362880))))
    )
    cosine = 1.0 + square * (
        -0.5 + square * (1.0 / 24 + square * (-1.0 / 720 + square * (1.0 / 40320 - square * (1.0 / 3628800))))
    )
    sine, cosine = 2.0 * sine * cosine, 1.0 - 2.0 * sine * sine
    sine, cosine = 2.0 * sine * cosine, 1.0 - 2.0 * sine * sine
    return cosine, sine


def sincos_small(angle):
    square = angle * angle
    sine = angle * (1.0 + square * (-1.0 / 6 + square * (1.0 / 120 - square * (1.0 / 5040))))
    cosine = 1.0 + square * (-0.5 + square * (1.0 / 24 + square * (-1.0 / 720 + square * (1.0 / 40320))))
    return cosine, sine


def cmul(a, b):
    return (a[0] * b[0] - a[1] * b[1], a[0] * b[1] + a[1] * b[0])


def cadd(a, b):
    return (a[0] + b[0], a[1] + b[1])


def csub(a, b):
    return (a[0] - b[0], a[1] - b[1])


def dft4(a, sign):
    even, odd = cadd(a[0], a[2]), cadd(a[1], a[3])
    even_d, odd_d = csub(a[0], a[2]), csub(a[1], a[3])
    turned = (-odd_d[1], odd_d[0]) if sign > 0 else (odd_d[1], -odd_d[0])
    return [cadd(even, odd), cadd(even_d, turned), csub(even, odd), csub(even_d, turned)]


def dft16(v, sign):
    half = math.sqrt(0.5)
    firsts = [dft4([v[4 * n1 + n2] for n1 in range(4)], sign) for n2 in range(4)]
    out = [None] * 16
    for k1 in range(4):
        column = []
        for n2 in range(4):
            re, im = firsts[n2][k1]
            turn = n2 * k1
            if turn == 2:
                re, im = (
                    (half * (re - im), half * (re + im)) if sign > 0 else (half * (re + im), half * (im - re))
                )
            elif turn == 4:
                re, im = (-im, re) if sign > 0 else (im, -re)
            elif turn == 6:
                re, im = (
                    (-half * (re + im), half * (re - im)) if sign > 0 else (half * (im - re), -half * (re + im))
                )
            elif turn:
                angle = 2.0 * math.pi * turn / 16
                re, im = cmul((re, im), (math.cos(angle), sign * math.sin(angle)))
            column.append((re, im))
        for k2, value in enumerate(dft4(column, sign)):
            out[k1 + 4 * k2] = value
    return out


def split(value):
    high = value.astype(jnp.bfloat16)
    low = (value - high.astype(jnp.float32)).astype(jnp.bfloat16)
    return high, low


def dot3(a, b, dims):
    def one(x, y):
        return lax.dot_general(x, y, (dims, ((), ())), preferred_element_type=jnp.float32)

    return one(a[0], b[0]) + (one(a[0], b[1]) + one(a[1], b[0]))


def pupil_parts(freq_rows, freq_cols):
    radius = freq_rows * freq_rows + freq_cols * freq_cols
    inside = 100 * radius < 9 * N * N
    radius_norm = radius.astype(jnp.float32) * (1.0 / float((N // 2) ** 2))
    axial_root = jnp.sqrt(1.0 - jnp.minimum(radius_norm, 0.36))
    cosine, sine = sincos_cycles(THICKNESS * (axial_root - 1.0))
    scale = jnp.where(inside, 1.0 / float(N * N), 0.0)
    return scale * cosine, scale * sine


def kernel(
    tilts_hbm, index_ref, wide_hbm, narrow_hbm, col_hbm, row_hbm, out_ref,
    strip, incident, section, send_a, recv_a, send_b, recv_b, pupil,
    tilts, wide, narrow, col_twist, row_twist,
    gather_send, gather_recv, pass_send, pass_recv, line_sem, plane_sem, pair_sem, a_send, a_recv, b_send, b_recv, load_sems,
):
    group = lax.axis_index("group")
    me = lax.axis_index("rows")
    loads = [
        pltpu.make_async_copy(source, target, load_sems.at[place])
        for place, (source, target) in enumerate(
            [
                (tilts_hbm, tilts),
                (index_ref, strip.at[group]),
                (col_hbm, col_twist),
                (wide_hbm, wide),
                (narrow_hbm, narrow),
                (row_hbm, row_twist),
            ]
        )
    ]
    for load in loads:
        load.start()

    def table(ref, place):
        rows = pl.ds(place[0], place[1])
        return ref[0, rows, :], ref[1, rows, :]

    partner = group + 1 - 2 * lax.rem(group, 2)
    group_next, group_last = lax.rem(group + 2, GROUPS), lax.rem(group + 6, GROUPS)
    group_far = lax.rem(group + 4, GROUPS)
    other_next, other_last, other_far = (lax.rem(partner + step, GROUPS) for step in (2, 6, 4))
    place_z, place_x, place_y = me // 32, lax.rem(me // 8, 4), lax.rem(me, 8)
    peers_y = [me - place_y + lax.rem(place_y + step, 8) for step in (2, 6, 1, 7)]
    peers_x = [me + 8 * (lax.rem(place_x + step, 4) - place_x) for step in (2, 1, 3)]
    peer_z = me + 32 * (1 - 2 * place_z)

    def signal(sem, axis, peer):
        pl.semaphore_signal(sem, inc=1, device_id={axis: peer}, device_id_type=MESH)

    with jax.named_scope("greet"):
        barrier = pltpu.get_barrier_semaphore()
        for peer in (group_next, group_last, partner, other_next, other_last):
            signal(barrier, "group", peer)
        for peer in peers_y + peers_x + [peer_z]:
            signal(barrier, "rows", peer)
        pl.semaphore_wait(barrier, 13)

    half = STRIP // 2

    def piece(owner, rows, sems, slot, peer, own=False):
        return pltpu.make_async_remote_copy(
            src_ref=index_ref.at[rows, :] if own else strip.at[owner, rows, :],
            dst_ref=strip.at[owner, rows, :],
            send_sem=sems[0].at[slot],
            recv_sem=sems[1].at[slot],
            device_id={"group": peer},
            device_id_type=MESH,
        )

    gather_sems, pass_sems = (gather_send, gather_recv), (pass_send, pass_recv)
    whole, top, bottom = pl.ds(0, STRIP), pl.ds(0, half), pl.ds(half, half)
    copies = []

    def send(*args, own=False):
        copies.append(piece(*args, own=own))
        copies[-1].start()

    def receive(*args):
        piece(*args).wait_recv()

    with jax.named_scope("gather_start"):
        send(group, whole, gather_sems, 0, group_next, own=True)
        send(group, whole, gather_sems, 1, group_last, own=True)
        send(group, whole, pass_sems, 0, partner, own=True)
        for peer in peers_y[:2]:
            signal(line_sem, "rows", peer)

    with jax.named_scope("incident_pupil"):
        loads[0].wait()
        tilt_row, tilt_col = tilts[0, 0], tilts[0, 1]
        pos_row = me * STRIP + lax.broadcasted_iota(jnp.int32, (STRIP, HIGH), 0)
        pos_col = lax.broadcasted_iota(jnp.int32, (STRIP, HIGH), 1)
        base = tilt_row * pos_row + tilt_col * pos_col
        for y1 in range(LOW):
            residue = (base + tilt_col * (HIGH * y1)) & (N - 1)
            cosine, sine = sincos_cycles(residue.astype(jnp.float32) * (1.0 / N))
            incident[0, y1] = cosine
            incident[1, y1] = sine

        lane = lax.broadcasted_iota(jnp.int32, (ROWS, FOLD * STRIP), 1)
        natural = lax.broadcasted_iota(jnp.int32, (ROWS, FOLD * STRIP), 0) + ROWS * lax.rem(lane, STRIP)
        freq_rows = jnp.where(natural < N // 2, natural, natural - N)
        tile_me = me // SLOTS
        slot_me = lax.rem(me, SLOTS)
        freq_cols = tile_me * FOLD + lane // STRIP + LOW * (slot_me * SUB - BANDS // 2)
        for sub in range(SUB):
            real, imag = pupil_parts(freq_rows, freq_cols + LOW * sub)
            pupil[0, sub] = real
            pupil[1, sub] = imag

    with jax.named_scope("gather_wait"):
        receive(group_last, whole, gather_sems, 0, group_next)
        send(group_last, top, gather_sems, 2, group_next)
        send(group_last, top, pass_sems, 3, other_next)
        send(group_last, whole, pass_sems, 1, partner)
        receive(group_next, whole, gather_sems, 1, group_last)
        send(group_next, bottom, gather_sems, 3, group_last)
        send(group_next, bottom, pass_sems, 4, other_last)
        send(group_next, whole, pass_sems, 2, partner)
        pl.semaphore_wait(line_sem, 2)
        for peer in peers_x:
            signal(plane_sem, "rows", peer)
        pl.semaphore_wait(plane_sem, 3)
        signal(pair_sem, "rows", peer_z)
        receive(group_far, top, gather_sems, 2, group_next)
        receive(group_far, bottom, gather_sems, 3, group_last)
        pl.semaphore_wait(pair_sem, 1)
        for slot, (owner, rows) in enumerate(
            [(group, whole), (group_last, whole), (group_next, whole), (group_far, top), (group_far, bottom)]
        ):
            receive(owner, rows, pass_sems, slot, partner)
        for place in (1, 2, 3, 4, 5):
            loads[place].wait()

    with jax.named_scope("screen_dft16"):
        for part in range(STRIP // 8):
            rows = pl.ds(8 * part, 8)
            values = []
            for y1 in range(LOW):
                lanes = pl.ds(HIGH * (y1 % 2), HIGH)
                contrast = strip[y1 // 2, rows, lanes]
                screen = sincos_small(contrast * (2.0 * math.pi * THICKNESS))
                values.append(cmul(screen, (incident[0, y1, rows, :], incident[1, y1, rows, :])))
            values = dft16(values, -1)
            for kap in range(LOW):
                twist = (col_twist[0, pl.ds(kap, 1), :], -col_twist[1, pl.ds(kap, 1), :])
                real, imag = cmul(values[kap], twist)
                place = pl.ds(kap * STRIP + 8 * part, 8)
                section[place, pl.ds(0, HIGH)] = real
                section[place, pl.ds(HIGH, HIGH)] = imag

    with jax.named_scope("column_128"):
        lanes = FOLD * STRIP
        tiles = [split(section[pl.ds(tile * lanes, lanes), :]) for tile in range(TILES)]

    side = lax.rem(group, 2)
    rows_y = {
        step: lax.rem(place_y + (1 - side) * step + side * (8 - step), 8) for step in (4, 3, 5, 2, 6, 1, 7, 0)
    }
    rows_x = {step: 8 * lax.rem(place_x + step, 4) for step in (2, 1, 3, 0)}
    rows_z = {1: 32 * (1 - place_z), 0: 32 * place_z}
    peers = [rows_y[y] + (rows_x[x] + rows_z[z]) for y in rows_y for x in rows_x for z in rows_z if x or y or z]

    def exchange(source, target, send_sem, recv_sem):
        msg = source.shape[0] // ROWS
        here = pl.ds(me * msg, msg)
        for peer in peers:
            pltpu.make_async_remote_copy(
                src_ref=source.at[pl.ds(peer * msg, msg), :],
                dst_ref=target.at[here, :],
                send_sem=send_sem,
                recv_sem=recv_sem,
                device_id={"rows": peer},
                device_id_type=MESH,
            ).start()
        target[pl.ds(me * msg, msg), :] = source[pl.ds(me * msg, msg), :]
        every = pl.ds(0, (ROWS - 1) * msg)
        return pltpu.make_async_remote_copy(
            src_ref=source.at[every, :],
            dst_ref=target.at[every, :],
            send_sem=send_sem,
            recv_sem=recv_sem,
            device_id={"rows": peer_z},
            device_id_type=MESH,
        )

    exchanges = []
    for chunk, (start, size) in enumerate(CHUNK_ROWS):
        with jax.named_scope("column_exchange"):
            forward = table(wide, (COL_FWD[0] + start, size))
            for tile in range(TILES):
                send_a[chunk][pl.ds(tile * size, size), :] = dot3(forward, tiles[tile], ((1,), (1,)))
            exchanges.append(exchange(send_a[chunk], recv_a[chunk], a_send.at[chunk], a_recv.at[chunk]))

    twist_cos, twist_sin = row_twist[0], row_twist[1]
    for chunk, (first, last) in enumerate(CHUNKS):
        subs = last - first
        msg = 2 * subs
        with jax.named_scope("row_wait"):
            exchanges[chunk].wait_recv()
        with jax.named_scope("row_work"):
            got = recv_a[chunk]
            parts = [
                jnp.concatenate([got[pl.ds(part * subs + sub, ROWS, stride=msg), :] for part in range(2)], axis=0)
                for sub in range(subs)
            ]
            data = split(jnp.concatenate(parts, axis=1))
            data = dot3(table(narrow, ROW_FWD), data, ((1,), (0,)))
            parts = []
            for sub in range(subs):
                columns = slice(sub * lanes, (sub + 1) * lanes)
                value = cmul((data[:ROWS, columns], data[ROWS:, columns]), (twist_cos, -twist_sin))
                parts.append(jnp.concatenate(value, axis=1))
            data = dot3(split(jnp.concatenate(parts, axis=0)), table(wide, IN_FWD), ((1,), (0,)))
            parts = []
            for sub in range(subs):
                rows = slice(sub * ROWS, (sub + 1) * ROWS)
                mask = (pupil[0, first + sub], pupil[1, first + sub])
                parts.append(jnp.concatenate(cmul((data[rows, :lanes], data[rows, lanes:]), mask), axis=1))
            data = dot3(split(jnp.concatenate(parts, axis=0)), table(wide, IN_INV), ((1,), (0,)))
            parts = []
            for sub in range(subs):
                rows = slice(sub * ROWS, (sub + 1) * ROWS)
                value = cmul((data[rows, :lanes], data[rows, lanes:]), (twist_cos, twist_sin))
                parts.append(jnp.concatenate(value, axis=0))
            data = dot3(table(narrow, ROW_INV), split(jnp.concatenate(parts, axis=1)), ((1,), (0,)))
            for sub in range(subs):
                columns = slice(sub * lanes, (sub + 1) * lanes)
                for part in range(2):
                    place = pl.ds(part * subs + sub, ROWS, stride=msg)
                    send_b[chunk][place, :] = data[part * ROWS : (part + 1) * ROWS, columns]
        with jax.named_scope("row_exchange"):
            exchanges.append(exchange(send_b[chunk], recv_b[chunk], b_send.at[chunk], b_recv.at[chunk]))

    for chunk, (start, size) in enumerate(CHUNK_ROWS):
        with jax.named_scope("column_wait"):
            exchanges[len(CHUNKS) + chunk].wait_recv()
        with jax.named_scope("columns_back"):
            inverse = table(wide, (COL_INV[0] + start, size))
            for tile in range(TILES):
                data = split(recv_b[chunk][pl.ds(tile * size, size), :].T)
                value = dot3(data, inverse, ((1,), (0,)))
                place = pl.ds(tile * lanes, lanes)
                section[place, :] = value if chunk == 0 else section[place, :] + value
    with jax.named_scope("columns_last"):
        for part in range(STRIP // 8):
            values = []
            for kap in range(LOW):
                place = pl.ds(kap * STRIP + 8 * part, 8)
                twist = (col_twist[0, pl.ds(kap, 1), :], col_twist[1, pl.ds(kap, 1), :])
                values.append(cmul((section[place, pl.ds(0, HIGH)], section[place, pl.ds(HIGH, HIGH)]), twist))
            values = dft16(values, 1)
            for y1 in range(LOW):
                for plane in range(2):
                    out_ref[plane, pl.ds(8 * part, 8), pl.ds(HIGH * y1, HIGH)] = values[y1][plane]

    for copy in copies + exchanges:
        copy.wait_send()


def per_device(illum_tilts, index_layers, measured):
    wide, narrow, col_twist, row_twist = tables()
    vmem = pl.BlockSpec(memory_space=pltpu.VMEM)
    messages = [pltpu.VMEM((2 * (hi - lo) * ROWS, FOLD * STRIP), jnp.float32) for lo, hi in CHUNKS]
    field = pl.pallas_call(
        kernel,
        out_shape=jax.ShapeDtypeStruct((2, STRIP, N), jnp.float32),
        in_specs=[pl.BlockSpec(memory_space=pltpu.HBM)] * 6,
        out_specs=vmem,
        scratch_shapes=[
            pltpu.VMEM((GROUPS, STRIP, N // GROUPS), jnp.float32),
            pltpu.VMEM((2, LOW, STRIP, HIGH), jnp.float32),
            pltpu.VMEM((LOW * STRIP, 2 * HIGH), jnp.float32),
            messages,
            messages,
            messages,
            messages,
            pltpu.VMEM((2, SUB, ROWS, FOLD * STRIP), jnp.float32),
            pltpu.SMEM((1, 2), jnp.int32),
            pltpu.VMEM(wide.shape, jnp.bfloat16),
            pltpu.VMEM(narrow.shape, jnp.bfloat16),
            pltpu.VMEM(col_twist.shape, jnp.float32),
            pltpu.VMEM(row_twist.shape, jnp.float32),
            pltpu.SemaphoreType.DMA((4,)),
            pltpu.SemaphoreType.DMA((4,)),
            pltpu.SemaphoreType.DMA((5,)),
            pltpu.SemaphoreType.DMA((5,)),
            pltpu.SemaphoreType.REGULAR,
            pltpu.SemaphoreType.REGULAR,
            pltpu.SemaphoreType.REGULAR,
            pltpu.SemaphoreType.DMA((len(CHUNKS),)),
            pltpu.SemaphoreType.DMA((len(CHUNKS),)),
            pltpu.SemaphoreType.DMA((len(CHUNKS),)),
            pltpu.SemaphoreType.DMA((len(CHUNKS),)),
            pltpu.SemaphoreType.DMA((6,)),
        ],
        compiler_params=pltpu.CompilerParams(
            collective_id=0, has_side_effects=True, vmem_limit_bytes=60 * 1024 * 1024
        ),
    )(
        illum_tilts,
        index_layers[0],
        jnp.asarray(wide),
        jnp.asarray(narrow),
        jnp.asarray(col_twist),
        jnp.asarray(row_twist),
    )
    return field[None] - measured


def solution(mesh):
    return jax.shard_map(
        per_device,
        mesh=mesh,
        in_specs=(P("group", None), P(None, "rows", "group"), P("group", None, "rows", None)),
        out_specs=P("group", None, "rows", None),
        check_vma=False,
    )
```

```python
import math

import jax
import jax.numpy as jnp
import ml_dtypes
import numpy as np
from jax import lax
from jax.experimental import pallas as pl
from jax.experimental.pallas import tpu as pltpu
from jax.sharding import PartitionSpec as P

N = 2048
THICKNESS = 4.0
MESH = pl.DeviceIdType.MESH

GROUPS = 8
ROWS = 64
STRIP = N // ROWS
LOW = 16
HIGH = 128
BANDS = 80
SUB = 5
FOLD = 4
CHUNKS = ((0, 1), (1, 2), (2, 3), (3, 5))
TILES = LOW // FOLD
SLOTS = BANDS // SUB


def split_const(table):
    high = table.astype(ml_dtypes.bfloat16)
    low = (table - high.astype(np.float64)).astype(ml_dtypes.bfloat16)
    return high, low


def real_form(cosine, sine):
    return np.block([[cosine, -sine], [sine, cosine]])


def tables():
    two_pi = 2.0 * math.pi
    m = np.arange(BANDS) - BANDS // 2
    angle = two_pi * ((m[:, None] * np.arange(HIGH)[None, :]) % HIGH) / HIGH
    forward = real_form(np.cos(angle), -np.sin(angle)).reshape(2, SLOTS, SUB, 2 * HIGH)
    forward = forward.transpose(1, 0, 2, 3)
    inverse = real_form(np.cos(angle.T), np.sin(angle.T)).reshape(2 * HIGH, 2, SLOTS, SUB)
    inverse = inverse.transpose(2, 1, 3, 0)
    col_fwd, col_inv = (
        np.concatenate([table[:, :, lo:hi].reshape(-1, 2 * HIGH) for lo, hi in CHUNKS])
        for table in (forward, inverse)
    )
    step = np.arange(ROWS)
    angle = two_pi * ((step[:, None] * step[None, :]) % ROWS) / ROWS
    row_fwd = real_form(np.cos(angle), -np.sin(angle))
    row_inv = real_form(np.cos(angle), np.sin(angle))
    step = np.arange(STRIP)
    angle = two_pi * ((step[:, None] * step[None, :]) % STRIP) / STRIP
    eye = np.eye(FOLD)
    cosine, sine = np.kron(eye, np.cos(angle)), np.kron(eye, np.sin(angle))
    in_fwd = real_form(cosine, -sine).T
    in_inv = real_form(cosine, sine).T
    angle = two_pi * (np.arange(LOW)[:, None] * np.arange(HIGH)[None, :]) / N
    col_twist = np.stack([np.cos(angle), np.sin(angle)]).astype(np.float32)
    angle = two_pi * (np.arange(ROWS)[:, None] * np.arange(STRIP)[None, :]) / N
    row_twist = np.stack([np.tile(np.cos(angle), FOLD), np.tile(np.sin(angle), FOLD)]).astype(
        np.float32
    )
    wide = np.stack(split_const(np.concatenate([col_fwd, col_inv, in_fwd, in_inv])))
    narrow = np.stack(split_const(np.concatenate([row_fwd, row_inv])))
    return wide, narrow, col_twist, row_twist


CHUNK_ROWS = [(2 * SLOTS * lo, 2 * SLOTS * (hi - lo)) for lo, hi in CHUNKS]
COL_FWD = (0, 2 * BANDS)
COL_INV = (2 * BANDS, 2 * BANDS)
IN_FWD = (4 * BANDS, 2 * HIGH)
IN_INV = (4 * BANDS + 2 * HIGH, 2 * HIGH)
ROW_FWD = (0, 2 * ROWS)
ROW_INV = (2 * ROWS, 2 * ROWS)


def sincos_cycles(cycles):
    cycles = cycles - jnp.round(cycles)
    quarter = cycles * (0.5 * math.pi)
    square = quarter * quarter
    sine = quarter * (
        1.0 + square * (-1.0 / 6 + square * (1.0 / 120 + square * (-1.0 / 5040 + square * (1.0 / 362880))))
    )
    cosine = 1.0 + square * (
        -0.5 + square * (1.0 / 24 + square * (-1.0 / 720 + square * (1.0 / 40320 - square * (1.0 / 3628800))))
    )
    sine, cosine = 2.0 * sine * cosine, 1.0 - 2.0 * sine * sine
    sine, cosine = 2.0 * sine * cosine, 1.0 - 2.0 * sine * sine
    return cosine, sine


def sincos_small(angle):
    square = angle * angle
    sine = angle * (1.0 + square * (-1.0 / 6 + square * (1.0 / 120 - square * (1.0 / 5040))))
    cosine = 1.0 + square * (-0.5 + square * (1.0 / 24 + square * (-1.0 / 720 + square * (1.0 / 40320))))
    return cosine, sine


def cmul(a, b):
    return (a[0] * b[0] - a[1] * b[1], a[0] * b[1] + a[1] * b[0])


def cadd(a, b):
    return (a[0] + b[0], a[1] + b[1])


def csub(a, b):
    return (a[0] - b[0], a[1] - b[1])


def dft4(a, sign):
    even, odd = cadd(a[0], a[2]), cadd(a[1], a[3])
    even_d, odd_d = csub(a[0], a[2]), csub(a[1], a[3])
    turned = (-odd_d[1], odd_d[0]) if sign > 0 else (odd_d[1], -odd_d[0])
    return [cadd(even, odd), cadd(even_d, turned), csub(even, odd), csub(even_d, turned)]


def dft16(v, sign):
    half = math.sqrt(0.5)
    firsts = [dft4([v[4 * n1 + n2] for n1 in range(4)], sign) for n2 in range(4)]
    out = [None] * 16
    for k1 in range(4):
        column = []
        for n2 in range(4):
            re, im = firsts[n2][k1]
            turn = n2 * k1
            if turn == 2:
                re, im = (
                    (half * (re - im), half * (re + im)) if sign > 0 else (half * (re + im), half * (im - re))
                )
            elif turn == 4:
                re, im = (-im, re) if sign > 0 else (im, -re)
            elif turn == 6:
                re, im = (
                    (-half * (re + im), half * (re - im)) if sign > 0 else (half * (im - re), -half * (re + im))
                )
            elif turn:
                angle = 2.0 * math.pi * turn / 16
                re, im = cmul((re, im), (math.cos(angle), sign * math.sin(angle)))
            column.append((re, im))
        for k2, value in enumerate(dft4(column, sign)):
            out[k1 + 4 * k2] = value
    return out


def split(value):
    high = value.astype(jnp.bfloat16)
    low = (value - high.astype(jnp.float32)).astype(jnp.bfloat16)
    return high, low


def dot3(a, b, dims):
    def one(x, y):
        return lax.dot_general(x, y, (dims, ((), ())), preferred_element_type=jnp.float32)

    rows = a[0].shape[0]
    both = one(jnp.concatenate(a, axis=0), b[0])
    return both[:rows] + (both[rows:] + one(a[0], b[1]))


def pupil_parts(freq_rows, freq_cols):
    radius = freq_rows * freq_rows + freq_cols * freq_cols
    inside = 100 * radius < 9 * N * N
    radius_norm = radius.astype(jnp.float32) * (1.0 / float((N // 2) ** 2))
    axial_root = jnp.sqrt(1.0 - jnp.minimum(radius_norm, 0.36))
    cosine, sine = sincos_cycles(THICKNESS * (axial_root - 1.0))
    scale = jnp.where(inside, 1.0 / float(N * N), 0.0)
    return scale * cosine, scale * sine


def kernel(
    tilts_hbm, index_ref, wide_hbm, narrow_hbm, col_hbm, row_hbm, out_ref,
    strip, incident, section, send_a, recv_a, send_b, recv_b, pupil,
    tilts, wide, narrow, col_twist, row_twist,
    gather_send, gather_recv, pass_send, pass_recv, line_sem, plane_sem, pair_sem, a_send, a_recv, b_send, b_recv, load_sems,
):
    group = lax.axis_index("group")
    me = lax.axis_index("rows")

    def table(ref, place):
        rows = pl.ds(place[0], place[1])
        return ref[0, rows, :], ref[1, rows, :]

    partner = group + 1 - 2 * lax.rem(group, 2)
    group_next, group_last = lax.rem(group + 2, GROUPS), lax.rem(group + 6, GROUPS)
    group_far = lax.rem(group + 4, GROUPS)
    other_next, other_last, other_far = (lax.rem(partner + step, GROUPS) for step in (2, 6, 4))
    place_z, place_x, place_y = me // 32, lax.rem(me // 8, 4), lax.rem(me, 8)
    peers_y = [me - place_y + lax.rem(place_y + step, 8) for step in (2, 6, 1, 7)]
    peers_x = [me + 8 * (lax.rem(place_x + step, 4) - place_x) for step in (2, 1, 3)]
    peer_z = me + 32 * (1 - 2 * place_z)

    def signal(sem, axis, peer):
        pl.semaphore_signal(sem, inc=1, device_id={axis: peer}, device_id_type=MESH)

    with jax.named_scope("greet"):
        barrier = pltpu.get_barrier_semaphore()
        for peer in (group_next, group_last, partner, other_next, other_last):
            signal(barrier, "group", peer)
        for peer in peers_y + peers_x + [peer_z]:
            signal(barrier, "rows", peer)
        loads = [
            pltpu.make_async_copy(source, target, load_sems.at[place])
            for place, (source, target) in enumerate(
                [
                    (tilts_hbm, tilts),
                    (index_ref, strip.at[group]),
                    (col_hbm, col_twist),
                    (wide_hbm, wide),
                    (narrow_hbm, narrow),
                    (row_hbm, row_twist),
                ]
            )
        ]
        for load in loads:
            load.start()
        pl.semaphore_wait(barrier, 13)

    half = STRIP // 2

    def piece(owner, rows, sems, slot, peer):
        return pltpu.make_async_remote_copy(
            src_ref=strip.at[owner, rows, :],
            dst_ref=strip.at[owner, rows, :],
            send_sem=sems[0].at[slot],
            recv_sem=sems[1].at[slot],
            device_id={"group": peer},
            device_id_type=MESH,
        )

    gather_sems, pass_sems = (gather_send, gather_recv), (pass_send, pass_recv)
    whole, top, bottom = pl.ds(0, STRIP), pl.ds(0, half), pl.ds(half, half)
    copies = []

    def send(*args):
        copies.append(piece(*args))
        copies[-1].start()

    def receive(*args):
        piece(*args).wait_recv()

    def screen(owner, rows=whole):
        for side_half in range(2):
            contrast = strip[owner, rows, pl.ds(HIGH * side_half, HIGH)]
            y1 = 2 * owner + side_half
            value = (incident[0, y1, rows, :], incident[1, y1, rows, :])
            value = cmul(sincos_small(contrast * (2.0 * math.pi * THICKNESS)), value)
            incident[0, y1, rows, :] = value[0]
            incident[1, y1, rows, :] = value[1]

    with jax.named_scope("gather_start"):
        loads[1].wait()
        send(group, whole, gather_sems, 0, group_next)
        send(group, whole, gather_sems, 1, group_last)
        send(group, whole, pass_sems, 0, partner)
        for peer in peers_y[:2]:
            signal(line_sem, "rows", peer)

    with jax.named_scope("incident_pupil"):
        loads[0].wait()
        tilt_row, tilt_col = tilts[0, 0], tilts[0, 1]
        pos_row = me * STRIP + lax.broadcasted_iota(jnp.int32, (STRIP, HIGH), 0)
        pos_col = lax.broadcasted_iota(jnp.int32, (STRIP, HIGH), 1)
        base = tilt_row * pos_row + tilt_col * pos_col
        for y1 in range(LOW):
            residue = (base + tilt_col * (HIGH * y1)) & (N - 1)
            cosine, sine = sincos_cycles(residue.astype(jnp.float32) * (1.0 / N))
            incident[0, y1] = cosine
            incident[1, y1] = sine

        lane = lax.broadcasted_iota(jnp.int32, (ROWS, FOLD * STRIP), 1)
        natural = lax.broadcasted_iota(jnp.int32, (ROWS, FOLD * STRIP), 0) + ROWS * lax.rem(lane, STRIP)
        freq_rows = jnp.where(natural < N // 2, natural, natural - N)
        tile_me = me // SLOTS
        slot_me = lax.rem(me, SLOTS)
        freq_cols = tile_me * FOLD + lane // STRIP + LOW * (slot_me * SUB - BANDS // 2)
        for sub in range(SUB):
            real, imag = pupil_parts(freq_rows, freq_cols + LOW * sub)
            pupil[0, sub] = real
            pupil[1, sub] = imag

    with jax.named_scope("gather_wait"):
        pl.semaphore_wait(line_sem, 2)
        for peer in peers_x:
            signal(plane_sem, "rows", peer)
        receive(group_last, whole, gather_sems, 0, group_next)
        send(group_last, top, gather_sems, 2, group_next)
        send(group_last, top, pass_sems, 3, other_next)
        send(group_last, whole, pass_sems, 1, partner)
        receive(group_next, whole, gather_sems, 1, group_last)
        send(group_next, bottom, gather_sems, 3, group_last)
        send(group_next, bottom, pass_sems, 4, other_last)
        send(group_next, whole, pass_sems, 2, partner)
        pl.semaphore_wait(plane_sem, 3)
        signal(pair_sem, "rows", peer_z)
        for owner in (group, group_last, group_next):
            screen(owner)
        receive(partner, whole, pass_sems, 0, partner)
        screen(partner)
        receive(group_far, top, gather_sems, 2, group_next)
        receive(group_far, bottom, gather_sems, 3, group_last)
        screen(group_far)
        for slot, (owner, rows) in enumerate([(other_last, whole), (other_next, whole)]):
            receive(owner, rows, pass_sems, 1 + slot, partner)
            screen(owner)
        for slot, rows in enumerate((top, bottom)):
            receive(other_far, rows, pass_sems, 3 + slot, partner)
        screen(other_far)
        for place in (2, 3, 4, 5):
            loads[place].wait()

    with jax.named_scope("screen_dft16"):
        for part in range(STRIP // 8):
            rows = pl.ds(8 * part, 8)
            values = []
            for y1 in range(LOW):
                values.append((incident[0, y1, rows, :], incident[1, y1, rows, :]))
            values = dft16(values, -1)
            for kap in range(LOW):
                twist = (col_twist[0, pl.ds(kap, 1), :], -col_twist[1, pl.ds(kap, 1), :])
                real, imag = cmul(values[kap], twist)
                place = pl.ds(kap * STRIP + 8 * part, 8)
                section[place, pl.ds(0, HIGH)] = real
                section[place, pl.ds(HIGH, HIGH)] = imag

    with jax.named_scope("column_128"):
        lanes = FOLD * STRIP
        tiles = [split(section[pl.ds(tile * lanes, lanes), :]) for tile in range(TILES)]

    side = lax.rem(group, 2)
    rows_y = {
        step: lax.rem(place_y + (1 - side) * step + side * (8 - step), 8) for step in (4, 3, 5, 2, 6, 1, 7, 0)
    }
    rows_x = {step: 8 * lax.rem(place_x + step, 4) for step in (2, 1, 3, 0)}
    rows_z = {1: 32 * (1 - place_z), 0: 32 * place_z}
    peers = [rows_y[y] + (rows_x[x] + rows_z[z]) for y in rows_y for x in rows_x for z in rows_z if x or y or z]

    def exchange(source, target, send_sem, recv_sem):
        msg = source.shape[0] // ROWS
        here = pl.ds(me * msg, msg)
        for peer in peers:
            pltpu.make_async_remote_copy(
                src_ref=source.at[pl.ds(peer * msg, msg), :],
                dst_ref=target.at[here, :],
                send_sem=send_sem,
                recv_sem=recv_sem,
                device_id={"rows": peer},
                device_id_type=MESH,
            ).start()
        target[pl.ds(me * msg, msg), :] = source[pl.ds(me * msg, msg), :]
        every = pl.ds(0, (ROWS - 1) * msg)
        return pltpu.make_async_remote_copy(
            src_ref=source.at[every, :],
            dst_ref=target.at[every, :],
            send_sem=send_sem,
            recv_sem=recv_sem,
            device_id={"rows": peer_z},
            device_id_type=MESH,
        )

    pl.semaphore_wait(pair_sem, 1)
    exchanges = []
    for chunk, (start, size) in enumerate(CHUNK_ROWS):
        with jax.named_scope("column_exchange"):
            forward = table(wide, (COL_FWD[0] + start, size))
            for tile in range(TILES):
                send_a[chunk][pl.ds(tile * size, size), :] = dot3(forward, tiles[tile], ((1,), (1,)))
            exchanges.append(exchange(send_a[chunk], recv_a[chunk], a_send.at[chunk], a_recv.at[chunk]))

    twist_cos, twist_sin = row_twist[0], row_twist[1]
    for chunk, (first, last) in enumerate(CHUNKS):
        subs = last - first
        msg = 2 * subs
        with jax.named_scope("row_wait"):
            exchanges[chunk].wait_recv()
        with jax.named_scope("row_work"):
            got = recv_a[chunk]
            parts = [
                jnp.concatenate([got[pl.ds(part * subs + sub, ROWS, stride=msg), :] for part in range(2)], axis=0)
                for sub in range(subs)
            ]
            data = split(jnp.concatenate(parts, axis=1))
            data = dot3(table(narrow, ROW_FWD), data, ((1,), (0,)))
            parts = []
            for sub in range(subs):
                columns = slice(sub * lanes, (sub + 1) * lanes)
                value = cmul((data[:ROWS, columns], data[ROWS:, columns]), (twist_cos, -twist_sin))
                parts.append(jnp.concatenate(value, axis=1))
            data = dot3(split(jnp.concatenate(parts, axis=0)), table(wide, IN_FWD), ((1,), (0,)))
            parts = []
            for sub in range(subs):
                rows = slice(sub * ROWS, (sub + 1) * ROWS)
                mask = (pupil[0, first + sub], pupil[1, first + sub])
                parts.append(jnp.concatenate(cmul((data[rows, :lanes], data[rows, lanes:]), mask), axis=1))
            data = dot3(split(jnp.concatenate(parts, axis=0)), table(wide, IN_INV), ((1,), (0,)))
            parts = []
            for sub in range(subs):
                rows = slice(sub * ROWS, (sub + 1) * ROWS)
                value = cmul((data[rows, :lanes], data[rows, lanes:]), (twist_cos, twist_sin))
                parts.append(jnp.concatenate(value, axis=0))
            data = dot3(table(narrow, ROW_INV), split(jnp.concatenate(parts, axis=1)), ((1,), (0,)))
            for sub in range(subs):
                columns = slice(sub * lanes, (sub + 1) * lanes)
                for part in range(2):
                    place = pl.ds(part * subs + sub, ROWS, stride=msg)
                    send_b[chunk][place, :] = data[part * ROWS : (part + 1) * ROWS, columns]
        with jax.named_scope("row_exchange"):
            exchanges.append(exchange(send_b[chunk], recv_b[chunk], b_send.at[chunk], b_recv.at[chunk]))

    for chunk, (start, size) in enumerate(CHUNK_ROWS):
        with jax.named_scope("column_wait"):
            exchanges[len(CHUNKS) + chunk].wait_recv()
        with jax.named_scope("columns_back"):
            inverse = table(wide, (COL_INV[0] + start, size))
            for tile in range(TILES):
                data = split(recv_b[chunk][pl.ds(tile * size, size), :].T)
                value = dot3(data, inverse, ((1,), (0,)))
                place = pl.ds(tile * lanes, lanes)
                section[place, :] = value if chunk == 0 else section[place, :] + value
    with jax.named_scope("columns_last"):
        for part in range(STRIP // 8):
            values = []
            for kap in range(LOW):
                place = pl.ds(kap * STRIP + 8 * part, 8)
                twist = (col_twist[0, pl.ds(kap, 1), :], col_twist[1, pl.ds(kap, 1), :])
                values.append(cmul((section[place, pl.ds(0, HIGH)], section[place, pl.ds(HIGH, HIGH)]), twist))
            values = dft16(values, 1)
            for y1 in range(LOW):
                for plane in range(2):
                    out_ref[plane, pl.ds(8 * part, 8), pl.ds(HIGH * y1, HIGH)] = values[y1][plane]

    for copy in copies + exchanges:
        copy.wait_send()


def per_device(illum_tilts, index_layers, measured):
    wide, narrow, col_twist, row_twist = tables()
    vmem = pl.BlockSpec(memory_space=pltpu.VMEM)
    messages = [pltpu.VMEM((2 * (hi - lo) * ROWS, FOLD * STRIP), jnp.float32) for lo, hi in CHUNKS]
    field = pl.pallas_call(
        kernel,
        out_shape=jax.ShapeDtypeStruct((2, STRIP, N), jnp.float32),
        in_specs=[pl.BlockSpec(memory_space=pltpu.HBM)] * 6,
        out_specs=vmem,
        scratch_shapes=[
            pltpu.VMEM((GROUPS, STRIP, N // GROUPS), jnp.float32),
            pltpu.VMEM((2, LOW, STRIP, HIGH), jnp.float32),
            pltpu.VMEM((LOW * STRIP, 2 * HIGH), jnp.float32),
            messages,
            messages,
            messages,
            messages,
            pltpu.VMEM((2, SUB, ROWS, FOLD * STRIP), jnp.float32),
            pltpu.SMEM((1, 2), jnp.int32),
            pltpu.VMEM(wide.shape, jnp.bfloat16),
            pltpu.VMEM(narrow.shape, jnp.bfloat16),
            pltpu.VMEM(col_twist.shape, jnp.float32),
            pltpu.VMEM(row_twist.shape, jnp.float32),
            pltpu.SemaphoreType.DMA((4,)),
            pltpu.SemaphoreType.DMA((4,)),
            pltpu.SemaphoreType.DMA((5,)),
            pltpu.SemaphoreType.DMA((5,)),
            pltpu.SemaphoreType.REGULAR,
            pltpu.SemaphoreType.REGULAR,
            pltpu.SemaphoreType.REGULAR,
            pltpu.SemaphoreType.DMA((len(CHUNKS),)),
            pltpu.SemaphoreType.DMA((len(CHUNKS),)),
            pltpu.SemaphoreType.DMA((len(CHUNKS),)),
            pltpu.SemaphoreType.DMA((len(CHUNKS),)),
            pltpu.SemaphoreType.DMA((6,)),
        ],
        compiler_params=pltpu.CompilerParams(
            collective_id=0, has_side_effects=True, vmem_limit_bytes=60 * 1024 * 1024
        ),
    )(
        illum_tilts,
        index_layers[0],
        jnp.asarray(wide),
        jnp.asarray(narrow),
        jnp.asarray(col_twist),
        jnp.asarray(row_twist),
    )
    return field[None] - measured


def solution(mesh):
    return jax.shard_map(
        per_device,
        mesh=mesh,
        in_specs=(P("group", None), P(None, "rows", "group"), P("group", None, "rows", None)),
        out_specs=P("group", None, "rows", None),
        check_vma=False,
    )
```

```python
import math

import jax
import jax.numpy as jnp
import ml_dtypes
import numpy as np
from jax import lax
from jax.experimental import pallas as pl
from jax.experimental.pallas import tpu as pltpu
from jax.sharding import PartitionSpec as P

N = 2048
THICKNESS = 4.0
MESH = pl.DeviceIdType.MESH

GROUPS = 8
ROWS = 64
STRIP = N // ROWS
LOW = 16
HIGH = 128
BANDS = 80
SUB = 5
FOLD = 4
CHUNKS = ((0, 1), (1, 2), (2, 3), (3, 5))
TILES = LOW // FOLD
SLOTS = BANDS // SUB


def split_const(table):
    high = table.astype(ml_dtypes.bfloat16)
    low = (table - high.astype(np.float64)).astype(ml_dtypes.bfloat16)
    return high, low


def real_form(cosine, sine):
    return np.block([[cosine, -sine], [sine, cosine]])


def tables():
    two_pi = 2.0 * math.pi
    m = np.arange(BANDS) - BANDS // 2
    angle = two_pi * ((m[:, None] * np.arange(HIGH)[None, :]) % HIGH) / HIGH
    forward = real_form(np.cos(angle), -np.sin(angle)).reshape(2, SLOTS, SUB, 2 * HIGH)
    forward = forward.transpose(1, 0, 2, 3)
    inverse = real_form(np.cos(angle.T), np.sin(angle.T)).reshape(2 * HIGH, 2, SLOTS, SUB)
    inverse = inverse.transpose(2, 1, 3, 0)
    col_fwd, col_inv = (
        np.concatenate([table[:, :, lo:hi].reshape(-1, 2 * HIGH) for lo, hi in CHUNKS])
        for table in (forward, inverse)
    )
    step = np.arange(ROWS)
    angle = two_pi * ((step[:, None] * step[None, :]) % ROWS) / ROWS
    row_fwd = real_form(np.cos(angle), -np.sin(angle))
    row_inv = real_form(np.cos(angle), np.sin(angle))
    step = np.arange(STRIP)
    angle = two_pi * ((step[:, None] * step[None, :]) % STRIP) / STRIP
    eye = np.eye(FOLD)
    cosine, sine = np.kron(eye, np.cos(angle)), np.kron(eye, np.sin(angle))
    in_fwd = real_form(cosine, -sine).T
    in_inv = real_form(cosine, sine).T
    angle = two_pi * (np.arange(LOW)[:, None] * np.arange(HIGH)[None, :]) / N
    col_twist = np.stack([np.cos(angle), np.sin(angle)]).astype(np.float32)
    angle = two_pi * (np.arange(ROWS)[:, None] * np.arange(STRIP)[None, :]) / N
    row_twist = np.stack([np.tile(np.cos(angle), FOLD), np.tile(np.sin(angle), FOLD)]).astype(
        np.float32
    )
    wide = np.stack(split_const(np.concatenate([col_fwd, col_inv, in_fwd, in_inv])))
    narrow = np.stack(split_const(np.concatenate([row_fwd, row_inv])))
    return wide, narrow, col_twist, row_twist


CHUNK_ROWS = [(2 * SLOTS * lo, 2 * SLOTS * (hi - lo)) for lo, hi in CHUNKS]
COL_FWD = (0, 2 * BANDS)
COL_INV = (2 * BANDS, 2 * BANDS)
IN_FWD = (4 * BANDS, 2 * HIGH)
IN_INV = (4 * BANDS + 2 * HIGH, 2 * HIGH)
ROW_FWD = (0, 2 * ROWS)
ROW_INV = (2 * ROWS, 2 * ROWS)


def sincos_cycles(cycles):
    cycles = cycles - jnp.round(cycles)
    quarter = cycles * (0.5 * math.pi)
    square = quarter * quarter
    sine = quarter * (
        1.0 + square * (-1.0 / 6 + square * (1.0 / 120 + square * (-1.0 / 5040 + square * (1.0 / 362880))))
    )
    cosine = 1.0 + square * (
        -0.5 + square * (1.0 / 24 + square * (-1.0 / 720 + square * (1.0 / 40320 - square * (1.0 / 3628800))))
    )
    sine, cosine = 2.0 * sine * cosine, 1.0 - 2.0 * sine * sine
    sine, cosine = 2.0 * sine * cosine, 1.0 - 2.0 * sine * sine
    return cosine, sine


def sincos_small(angle):
    square = angle * angle
    sine = angle * (1.0 + square * (-1.0 / 6 + square * (1.0 / 120 - square * (1.0 / 5040))))
    cosine = 1.0 + square * (-0.5 + square * (1.0 / 24 + square * (-1.0 / 720 + square * (1.0 / 40320))))
    return cosine, sine


def cmul(a, b):
    return (a[0] * b[0] - a[1] * b[1], a[0] * b[1] + a[1] * b[0])


def cadd(a, b):
    return (a[0] + b[0], a[1] + b[1])


def csub(a, b):
    return (a[0] - b[0], a[1] - b[1])


def dft4(a, sign):
    even, odd = cadd(a[0], a[2]), cadd(a[1], a[3])
    even_d, odd_d = csub(a[0], a[2]), csub(a[1], a[3])
    turned = (-odd_d[1], odd_d[0]) if sign > 0 else (odd_d[1], -odd_d[0])
    return [cadd(even, odd), cadd(even_d, turned), csub(even, odd), csub(even_d, turned)]


def dft16(v, sign):
    half = math.sqrt(0.5)
    firsts = [dft4([v[4 * n1 + n2] for n1 in range(4)], sign) for n2 in range(4)]
    out = [None] * 16
    for k1 in range(4):
        column = []
        for n2 in range(4):
            re, im = firsts[n2][k1]
            turn = n2 * k1
            if turn == 2:
                re, im = (
                    (half * (re - im), half * (re + im)) if sign > 0 else (half * (re + im), half * (im - re))
                )
            elif turn == 4:
                re, im = (-im, re) if sign > 0 else (im, -re)
            elif turn == 6:
                re, im = (
                    (-half * (re + im), half * (re - im)) if sign > 0 else (half * (im - re), -half * (re + im))
                )
            elif turn:
                angle = 2.0 * math.pi * turn / 16
                re, im = cmul((re, im), (math.cos(angle), sign * math.sin(angle)))
            column.append((re, im))
        for k2, value in enumerate(dft4(column, sign)):
            out[k1 + 4 * k2] = value
    return out


def split(value):
    high = value.astype(jnp.bfloat16)
    low = (value - high.astype(jnp.float32)).astype(jnp.bfloat16)
    return high, low


def dot3(a, b, dims):
    def one(x, y):
        return lax.dot_general(x, y, (dims, ((), ())), preferred_element_type=jnp.float32)

    rows = a[0].shape[0]
    both = one(jnp.concatenate(a, axis=0), b[0])
    return both[:rows] + (both[rows:] + one(a[0], b[1]))


def pupil_parts(freq_rows, freq_cols):
    radius = freq_rows * freq_rows + freq_cols * freq_cols
    inside = 100 * radius < 9 * N * N
    radius_norm = radius.astype(jnp.float32) * (1.0 / float((N // 2) ** 2))
    axial_root = jnp.sqrt(1.0 - jnp.minimum(radius_norm, 0.36))
    cosine, sine = sincos_cycles(THICKNESS * (axial_root - 1.0))
    scale = jnp.where(inside, 1.0 / float(N * N), 0.0)
    return scale * cosine, scale * sine


def kernel(
    tilts_hbm, index_ref, wide_hbm, narrow_hbm, col_hbm, row_hbm, out_hbm,
    strip, incident, section, send_a, recv_a, send_b, recv_b, pupil,
    tilts, wide, narrow, col_twist, row_twist, out_ref, out_sems,
    gather_send, gather_recv, pass_send, pass_recv, line_sem, plane_sem, pair_sem, a_send, a_recv, b_send, b_recv, load_sems,
):
    group = lax.axis_index("group")
    me = lax.axis_index("rows")

    def table(ref, place):
        rows = pl.ds(place[0], place[1])
        return ref[0, rows, :], ref[1, rows, :]

    partner = group + 1 - 2 * lax.rem(group, 2)
    group_next, group_last = lax.rem(group + 2, GROUPS), lax.rem(group + 6, GROUPS)
    group_far = lax.rem(group + 4, GROUPS)
    other_next, other_last, other_far = (lax.rem(partner + step, GROUPS) for step in (2, 6, 4))
    place_z, place_x, place_y = me // 32, lax.rem(me // 8, 4), lax.rem(me, 8)
    peers_y = [me - place_y + lax.rem(place_y + step, 8) for step in (2, 6, 1, 7)]
    peers_x = [me + 8 * (lax.rem(place_x + step, 4) - place_x) for step in (2, 1, 3)]
    peer_z = me + 32 * (1 - 2 * place_z)

    def signal(sem, axis, peer):
        pl.semaphore_signal(sem, inc=1, device_id={axis: peer}, device_id_type=MESH)

    with jax.named_scope("greet"):
        barrier = pltpu.get_barrier_semaphore()
        for peer in (group_next, group_last, partner, other_next, other_last):
            signal(barrier, "group", peer)
        for peer in peers_y + peers_x + [peer_z]:
            signal(barrier, "rows", peer)
        loads = [
            pltpu.make_async_copy(source, target, load_sems.at[place])
            for place, (source, target) in enumerate(
                [
                    (tilts_hbm, tilts),
                    (index_ref, strip.at[group]),
                    (col_hbm, col_twist),
                    (wide_hbm, wide),
                    (narrow_hbm, narrow),
                    (row_hbm, row_twist),
                ]
            )
        ]
        for load in loads:
            load.start()
        pl.semaphore_wait(barrier, 13)

    half = STRIP // 2

    def piece(owner, rows, sems, slot, peer):
        return pltpu.make_async_remote_copy(
            src_ref=strip.at[owner, rows, :],
            dst_ref=strip.at[owner, rows, :],
            send_sem=sems[0].at[slot],
            recv_sem=sems[1].at[slot],
            device_id={"group": peer},
            device_id_type=MESH,
        )

    gather_sems, pass_sems = (gather_send, gather_recv), (pass_send, pass_recv)
    whole, top, bottom = pl.ds(0, STRIP), pl.ds(0, half), pl.ds(half, half)
    copies = []

    def send(*args):
        copies.append(piece(*args))
        copies[-1].start()

    def receive(*args):
        piece(*args).wait_recv()

    def screen(owner, rows=whole):
        for side_half in range(2):
            contrast = strip[owner, rows, pl.ds(HIGH * side_half, HIGH)]
            y1 = 2 * owner + side_half
            value = (incident[0, y1, rows, :], incident[1, y1, rows, :])
            value = cmul(sincos_small(contrast * (2.0 * math.pi * THICKNESS)), value)
            incident[0, y1, rows, :] = value[0]
            incident[1, y1, rows, :] = value[1]

    with jax.named_scope("gather_start"):
        loads[1].wait()
        send(group, whole, gather_sems, 0, group_next)
        send(group, whole, gather_sems, 1, group_last)
        send(group, whole, pass_sems, 0, partner)
        for peer in peers_y[:2]:
            signal(line_sem, "rows", peer)

    with jax.named_scope("incident_pupil"):
        loads[0].wait()
        tilt_row, tilt_col = tilts[0, 0], tilts[0, 1]
        pos_row = me * STRIP + lax.broadcasted_iota(jnp.int32, (STRIP, HIGH), 0)
        pos_col = lax.broadcasted_iota(jnp.int32, (STRIP, HIGH), 1)
        base = tilt_row * pos_row + tilt_col * pos_col
        for y1 in range(LOW):
            residue = (base + tilt_col * (HIGH * y1)) & (N - 1)
            cosine, sine = sincos_cycles(residue.astype(jnp.float32) * (1.0 / N))
            incident[0, y1] = cosine
            incident[1, y1] = sine

        lane = lax.broadcasted_iota(jnp.int32, (ROWS, FOLD * STRIP), 1)
        natural = lax.broadcasted_iota(jnp.int32, (ROWS, FOLD * STRIP), 0) + ROWS * lax.rem(lane, STRIP)
        freq_rows = jnp.where(natural < N // 2, natural, natural - N)
        tile_me = me // SLOTS
        slot_me = lax.rem(me, SLOTS)
        freq_cols = tile_me * FOLD + lane // STRIP + LOW * (slot_me * SUB - BANDS // 2)
        for sub in range(SUB):
            real, imag = pupil_parts(freq_rows, freq_cols + LOW * sub)
            pupil[0, sub] = real
            pupil[1, sub] = imag

    with jax.named_scope("gather_wait"):
        pl.semaphore_wait(line_sem, 2)
        for peer in peers_x:
            signal(plane_sem, "rows", peer)
        receive(group_last, whole, gather_sems, 0, group_next)
        send(group_last, top, gather_sems, 2, group_next)
        send(group_last, top, pass_sems, 3, other_next)
        send(group_last, whole, pass_sems, 1, partner)
        receive(group_next, whole, gather_sems, 1, group_last)
        send(group_next, bottom, gather_sems, 3, group_last)
        send(group_next, bottom, pass_sems, 4, other_last)
        send(group_next, whole, pass_sems, 2, partner)
        pl.semaphore_wait(plane_sem, 3)
        signal(pair_sem, "rows", peer_z)
        for owner in (group, group_last, group_next):
            screen(owner)
        receive(partner, whole, pass_sems, 0, partner)
        screen(partner)
        receive(group_far, top, gather_sems, 2, group_next)
        receive(group_far, bottom, gather_sems, 3, group_last)
        screen(group_far)
        for slot, (owner, rows) in enumerate([(other_last, whole), (other_next, whole)]):
            receive(owner, rows, pass_sems, 1 + slot, partner)
            screen(owner)
        for slot, rows in enumerate((top, bottom)):
            receive(other_far, rows, pass_sems, 3 + slot, partner)
        screen(other_far)
        for place in (2, 3, 4, 5):
            loads[place].wait()

    with jax.named_scope("screen_dft16"):
        for part in range(STRIP // 8):
            rows = pl.ds(8 * part, 8)
            values = []
            for y1 in range(LOW):
                values.append((incident[0, y1, rows, :], incident[1, y1, rows, :]))
            values = dft16(values, -1)
            for kap in range(LOW):
                twist = (col_twist[0, pl.ds(kap, 1), :], -col_twist[1, pl.ds(kap, 1), :])
                real, imag = cmul(values[kap], twist)
                place = pl.ds(kap * STRIP + 8 * part, 8)
                section[place, pl.ds(0, HIGH)] = real
                section[place, pl.ds(HIGH, HIGH)] = imag

    with jax.named_scope("column_128"):
        lanes = FOLD * STRIP
        tiles = [split(section[pl.ds(tile * lanes, lanes), :]) for tile in range(TILES)]

    side = lax.rem(group, 2)
    rows_y = {
        step: lax.rem(place_y + (1 - side) * step + side * (8 - step), 8) for step in (4, 3, 5, 2, 6, 1, 7, 0)
    }
    rows_x = {step: 8 * lax.rem(place_x + step, 4) for step in (2, 1, 3, 0)}
    rows_z = {1: 32 * (1 - place_z), 0: 32 * place_z}
    peers = [rows_y[y] + (rows_x[x] + rows_z[z]) for y in rows_y for x in rows_x for z in rows_z if x or y or z]

    def exchange(source, target, send_sem, recv_sem):
        msg = source.shape[0] // ROWS
        here = pl.ds(me * msg, msg)
        for peer in peers:
            pltpu.make_async_remote_copy(
                src_ref=source.at[pl.ds(peer * msg, msg), :],
                dst_ref=target.at[here, :],
                send_sem=send_sem,
                recv_sem=recv_sem,
                device_id={"rows": peer},
                device_id_type=MESH,
            ).start()
        target[pl.ds(me * msg, msg), :] = source[pl.ds(me * msg, msg), :]
        every = pl.ds(0, (ROWS - 1) * msg)
        return pltpu.make_async_remote_copy(
            src_ref=source.at[every, :],
            dst_ref=target.at[every, :],
            send_sem=send_sem,
            recv_sem=recv_sem,
            device_id={"rows": peer_z},
            device_id_type=MESH,
        )

    pl.semaphore_wait(pair_sem, 1)
    exchanges = []
    for chunk, (start, size) in enumerate(CHUNK_ROWS):
        with jax.named_scope("column_exchange"):
            forward = table(wide, (COL_FWD[0] + start, size))
            for tile in range(TILES):
                send_a[chunk][pl.ds(tile * size, size), :] = dot3(forward, tiles[tile], ((1,), (1,)))
            exchanges.append(exchange(send_a[chunk], recv_a[chunk], a_send.at[chunk], a_recv.at[chunk]))

    twist_cos, twist_sin = row_twist[0], row_twist[1]
    for chunk, (first, last) in enumerate(CHUNKS):
        subs = last - first
        msg = 2 * subs
        with jax.named_scope("row_wait"):
            exchanges[chunk].wait_recv()
        with jax.named_scope("row_work"):
            got = recv_a[chunk]
            parts = [
                jnp.concatenate([got[pl.ds(part * subs + sub, ROWS, stride=msg), :] for part in range(2)], axis=0)
                for sub in range(subs)
            ]
            data = split(jnp.concatenate(parts, axis=1))
            data = dot3(table(narrow, ROW_FWD), data, ((1,), (0,)))
            parts = []
            for sub in range(subs):
                columns = slice(sub * lanes, (sub + 1) * lanes)
                value = cmul((data[:ROWS, columns], data[ROWS:, columns]), (twist_cos, -twist_sin))
                parts.append(jnp.concatenate(value, axis=1))
            data = dot3(split(jnp.concatenate(parts, axis=0)), table(wide, IN_FWD), ((1,), (0,)))
            parts = []
            for sub in range(subs):
                rows = slice(sub * ROWS, (sub + 1) * ROWS)
                mask = (pupil[0, first + sub], pupil[1, first + sub])
                parts.append(jnp.concatenate(cmul((data[rows, :lanes], data[rows, lanes:]), mask), axis=1))
            data = dot3(split(jnp.concatenate(parts, axis=0)), table(wide, IN_INV), ((1,), (0,)))
            parts = []
            for sub in range(subs):
                rows = slice(sub * ROWS, (sub + 1) * ROWS)
                value = cmul((data[rows, :lanes], data[rows, lanes:]), (twist_cos, twist_sin))
                parts.append(jnp.concatenate(value, axis=0))
            data = dot3(table(narrow, ROW_INV), split(jnp.concatenate(parts, axis=1)), ((1,), (0,)))
            for sub in range(subs):
                columns = slice(sub * lanes, (sub + 1) * lanes)
                for part in range(2):
                    place = pl.ds(part * subs + sub, ROWS, stride=msg)
                    send_b[chunk][place, :] = data[part * ROWS : (part + 1) * ROWS, columns]
        with jax.named_scope("row_exchange"):
            exchanges.append(exchange(send_b[chunk], recv_b[chunk], b_send.at[chunk], b_recv.at[chunk]))

    for chunk, (start, size) in enumerate(CHUNK_ROWS):
        with jax.named_scope("column_wait"):
            exchanges[len(CHUNKS) + chunk].wait_recv()
        with jax.named_scope("columns_back"):
            inverse = table(wide, (COL_INV[0] + start, size))
            for tile in range(TILES):
                data = split(recv_b[chunk][pl.ds(tile * size, size), :].T)
                value = dot3(data, inverse, ((1,), (0,)))
                place = pl.ds(tile * lanes, lanes)
                section[place, :] = value if chunk == 0 else section[place, :] + value
    results = []
    with jax.named_scope("columns_last"):
        for part in range(STRIP // 8):
            values = []
            for kap in range(LOW):
                place = pl.ds(kap * STRIP + 8 * part, 8)
                twist = (col_twist[0, pl.ds(kap, 1), :], col_twist[1, pl.ds(kap, 1), :])
                values.append(cmul((section[place, pl.ds(0, HIGH)], section[place, pl.ds(HIGH, HIGH)]), twist))
            values = dft16(values, 1)
            for y1 in range(LOW):
                for plane in range(2):
                    out_ref[plane, pl.ds(8 * part, 8), pl.ds(HIGH * y1, HIGH)] = values[y1][plane]
            rows = pl.ds(8 * part, 8)
            results.append(pltpu.make_async_copy(out_ref.at[:, rows, :], out_hbm.at[:, rows, :], out_sems.at[part]))
            results[-1].start()

    for copy in copies + exchanges:
        copy.wait_send()
    for copy in results:
        copy.wait()


def per_device(illum_tilts, index_layers, measured):
    wide, narrow, col_twist, row_twist = tables()
    messages = [pltpu.VMEM((2 * (hi - lo) * ROWS, FOLD * STRIP), jnp.float32) for lo, hi in CHUNKS]
    field = pl.pallas_call(
        kernel,
        out_shape=jax.ShapeDtypeStruct((2, STRIP, N), jnp.float32),
        in_specs=[pl.BlockSpec(memory_space=pltpu.HBM)] * 6,
        out_specs=pl.BlockSpec(memory_space=pltpu.HBM),
        scratch_shapes=[
            pltpu.VMEM((GROUPS, STRIP, N // GROUPS), jnp.float32),
            pltpu.VMEM((2, LOW, STRIP, HIGH), jnp.float32),
            pltpu.VMEM((LOW * STRIP, 2 * HIGH), jnp.float32),
            messages,
            messages,
            messages,
            messages,
            pltpu.VMEM((2, SUB, ROWS, FOLD * STRIP), jnp.float32),
            pltpu.SMEM((1, 2), jnp.int32),
            pltpu.VMEM(wide.shape, jnp.bfloat16),
            pltpu.VMEM(narrow.shape, jnp.bfloat16),
            pltpu.VMEM(col_twist.shape, jnp.float32),
            pltpu.VMEM(row_twist.shape, jnp.float32),
            pltpu.VMEM((2, STRIP, N), jnp.float32),
            pltpu.SemaphoreType.DMA((STRIP // 8,)),
            pltpu.SemaphoreType.DMA((4,)),
            pltpu.SemaphoreType.DMA((4,)),
            pltpu.SemaphoreType.DMA((5,)),
            pltpu.SemaphoreType.DMA((5,)),
            pltpu.SemaphoreType.REGULAR,
            pltpu.SemaphoreType.REGULAR,
            pltpu.SemaphoreType.REGULAR,
            pltpu.SemaphoreType.DMA((len(CHUNKS),)),
            pltpu.SemaphoreType.DMA((len(CHUNKS),)),
            pltpu.SemaphoreType.DMA((len(CHUNKS),)),
            pltpu.SemaphoreType.DMA((len(CHUNKS),)),
            pltpu.SemaphoreType.DMA((6,)),
        ],
        compiler_params=pltpu.CompilerParams(
            collective_id=0, has_side_effects=True, vmem_limit_bytes=60 * 1024 * 1024
        ),
    )(
        illum_tilts,
        index_layers[0],
        jnp.asarray(wide),
        jnp.asarray(narrow),
        jnp.asarray(col_twist),
        jnp.asarray(row_twist),
    )
    return field[None] - measured


def solution(mesh):
    return jax.shard_map(
        per_device,
        mesh=mesh,
        in_specs=(P("group", None), P(None, "rows", "group"), P("group", None, "rows", None)),
        out_specs=P("group", None, "rows", None),
        check_vma=False,
    )
```

```python
import math

import jax
import jax.numpy as jnp
import ml_dtypes
import numpy as np
from jax import lax
from jax.experimental import pallas as pl
from jax.experimental.pallas import tpu as pltpu
from jax.sharding import PartitionSpec as P

N = 2048
THICKNESS = 4.0
MESH = pl.DeviceIdType.MESH

GROUPS = 8
ROWS = 64
STRIP = N // ROWS
LOW = 16
HIGH = 128
BANDS = 80
SUB = 5
FOLD = 4
CHUNKS = ((0, 1), (1, 3), (3, 5))
TILES = LOW // FOLD
SLOTS = BANDS // SUB


def split_const(table):
    high = table.astype(ml_dtypes.bfloat16)
    low = (table - high.astype(np.float64)).astype(ml_dtypes.bfloat16)
    return high, low


def real_form(cosine, sine):
    return np.block([[cosine, -sine], [sine, cosine]])


def tables():
    two_pi = 2.0 * math.pi
    m = np.arange(BANDS) - BANDS // 2
    angle = two_pi * ((m[:, None] * np.arange(HIGH)[None, :]) % HIGH) / HIGH
    forward = real_form(np.cos(angle), -np.sin(angle)).reshape(2, SLOTS, SUB, 2 * HIGH)
    forward = forward.transpose(1, 0, 2, 3)
    inverse = real_form(np.cos(angle.T), np.sin(angle.T)).reshape(2 * HIGH, 2, SLOTS, SUB)
    inverse = inverse.transpose(2, 1, 3, 0)
    col_fwd, col_inv = (
        np.concatenate([table[:, :, lo:hi].reshape(-1, 2 * HIGH) for lo, hi in CHUNKS])
        for table in (forward, inverse)
    )
    step = np.arange(ROWS)
    angle = two_pi * ((step[:, None] * step[None, :]) % ROWS) / ROWS
    row_fwd = real_form(np.cos(angle), -np.sin(angle))
    row_inv = real_form(np.cos(angle), np.sin(angle))
    step = np.arange(STRIP)
    angle = two_pi * ((step[:, None] * step[None, :]) % STRIP) / STRIP
    eye = np.eye(FOLD)
    cosine, sine = np.kron(eye, np.cos(angle)), np.kron(eye, np.sin(angle))
    in_fwd = real_form(cosine, -sine).T
    in_inv = real_form(cosine, sine).T
    angle = two_pi * (np.arange(LOW)[:, None] * np.arange(HIGH)[None, :]) / N
    col_twist = np.stack([np.cos(angle), np.sin(angle)]).astype(np.float32)
    angle = two_pi * (np.arange(ROWS)[:, None] * np.arange(STRIP)[None, :]) / N
    row_twist = np.stack([np.tile(np.cos(angle), FOLD), np.tile(np.sin(angle), FOLD)]).astype(
        np.float32
    )
    wide = np.stack(split_const(np.concatenate([col_fwd, col_inv, in_fwd, in_inv])))
    narrow = np.stack(split_const(np.concatenate([row_fwd, row_inv])))
    return wide, narrow, col_twist, row_twist


CHUNK_ROWS = [(2 * SLOTS * lo, 2 * SLOTS * (hi - lo)) for lo, hi in CHUNKS]
COL_FWD = (0, 2 * BANDS)
COL_INV = (2 * BANDS, 2 * BANDS)
IN_FWD = (4 * BANDS, 2 * HIGH)
IN_INV = (4 * BANDS + 2 * HIGH, 2 * HIGH)
ROW_FWD = (0, 2 * ROWS)
ROW_INV = (2 * ROWS, 2 * ROWS)


def sincos_cycles(cycles):
    cycles = cycles - jnp.round(cycles)
    quarter = cycles * (0.5 * math.pi)
    square = quarter * quarter
    sine = quarter * (
        1.0 + square * (-1.0 / 6 + square * (1.0 / 120 + square * (-1.0 / 5040 + square * (1.0 / 362880))))
    )
    cosine = 1.0 + square * (
        -0.5 + square * (1.0 / 24 + square * (-1.0 / 720 + square * (1.0 / 40320 - square * (1.0 / 3628800))))
    )
    sine, cosine = 2.0 * sine * cosine, 1.0 - 2.0 * sine * sine
    sine, cosine = 2.0 * sine * cosine, 1.0 - 2.0 * sine * sine
    return cosine, sine


def sincos_small(angle):
    square = angle * angle
    sine = angle * (1.0 + square * (-1.0 / 6 + square * (1.0 / 120 - square * (1.0 / 5040))))
    cosine = 1.0 + square * (-0.5 + square * (1.0 / 24 + square * (-1.0 / 720 + square * (1.0 / 40320))))
    return cosine, sine


def cmul(a, b):
    return (a[0] * b[0] - a[1] * b[1], a[0] * b[1] + a[1] * b[0])


def cadd(a, b):
    return (a[0] + b[0], a[1] + b[1])


def csub(a, b):
    return (a[0] - b[0], a[1] - b[1])


def dft4(a, sign):
    even, odd = cadd(a[0], a[2]), cadd(a[1], a[3])
    even_d, odd_d = csub(a[0], a[2]), csub(a[1], a[3])
    turned = (-odd_d[1], odd_d[0]) if sign > 0 else (odd_d[1], -odd_d[0])
    return [cadd(even, odd), cadd(even_d, turned), csub(even, odd), csub(even_d, turned)]


def dft16(v, sign):
    half = math.sqrt(0.5)
    firsts = [dft4([v[4 * n1 + n2] for n1 in range(4)], sign) for n2 in range(4)]
    out = [None] * 16
    for k1 in range(4):
        column = []
        for n2 in range(4):
            re, im = firsts[n2][k1]
            turn = n2 * k1
            if turn == 2:
                re, im = (
                    (half * (re - im), half * (re + im)) if sign > 0 else (half * (re + im), half * (im - re))
                )
            elif turn == 4:
                re, im = (-im, re) if sign > 0 else (im, -re)
            elif turn == 6:
                re, im = (
                    (-half * (re + im), half * (re - im)) if sign > 0 else (half * (im - re), -half * (re + im))
                )
            elif turn:
                angle = 2.0 * math.pi * turn / 16
                re, im = cmul((re, im), (math.cos(angle), sign * math.sin(angle)))
            column.append((re, im))
        for k2, value in enumerate(dft4(column, sign)):
            out[k1 + 4 * k2] = value
    return out


def split(value):
    high = value.astype(jnp.bfloat16)
    low = (value - high.astype(jnp.float32)).astype(jnp.bfloat16)
    return high, low


def dot3(a, b, dims):
    def one(x, y):
        return lax.dot_general(x, y, (dims, ((), ())), preferred_element_type=jnp.float32)

    rows = a[0].shape[0]
    both = one(jnp.concatenate(a, axis=0), b[0])
    return both[:rows] + (both[rows:] + one(a[0], b[1]))


def pupil_parts(freq_rows, freq_cols):
    radius = freq_rows * freq_rows + freq_cols * freq_cols
    inside = 100 * radius < 9 * N * N
    radius_norm = radius.astype(jnp.float32) * (1.0 / float((N // 2) ** 2))
    axial_root = jnp.sqrt(1.0 - jnp.minimum(radius_norm, 0.36))
    cosine, sine = sincos_cycles(THICKNESS * (axial_root - 1.0))
    scale = jnp.where(inside, 1.0 / float(N * N), 0.0)
    return scale * cosine, scale * sine


def kernel(
    tilts_hbm, index_ref, wide_hbm, narrow_hbm, col_hbm, row_hbm, out_hbm,
    strip, incident, section, send_a, recv_a, send_b, recv_b, pupil,
    tilts, wide, narrow, col_twist, row_twist, out_ref, out_sems,
    gather_send, gather_recv, pass_send, pass_recv, line_sem, plane_sem, pair_sem, a_send, a_recv, b_send, b_recv, load_sems,
):
    group = lax.axis_index("group")
    me = lax.axis_index("rows")

    def table(ref, place):
        rows = pl.ds(place[0], place[1])
        return ref[0, rows, :], ref[1, rows, :]

    partner = group + 1 - 2 * lax.rem(group, 2)
    group_next, group_last = lax.rem(group + 2, GROUPS), lax.rem(group + 6, GROUPS)
    group_far = lax.rem(group + 4, GROUPS)
    other_next, other_last, other_far = (lax.rem(partner + step, GROUPS) for step in (2, 6, 4))
    place_z, place_x, place_y = me // 32, lax.rem(me // 8, 4), lax.rem(me, 8)
    peers_y = [me - place_y + lax.rem(place_y + step, 8) for step in (2, 6, 1, 7)]
    peers_x = [me + 8 * (lax.rem(place_x + step, 4) - place_x) for step in (2, 1, 3)]
    peer_z = me + 32 * (1 - 2 * place_z)

    def signal(sem, axis, peer):
        pl.semaphore_signal(sem, inc=1, device_id={axis: peer}, device_id_type=MESH)

    with jax.named_scope("greet"):
        barrier = pltpu.get_barrier_semaphore()
        for peer in (group_next, group_last, partner, other_next, other_last):
            signal(barrier, "group", peer)
        for peer in peers_y + peers_x + [peer_z]:
            signal(barrier, "rows", peer)
        loads = [
            pltpu.make_async_copy(source, target, load_sems.at[place])
            for place, (source, target) in enumerate(
                [
                    (tilts_hbm, tilts),
                    (index_ref, strip.at[group]),
                    (col_hbm, col_twist),
                    (wide_hbm, wide),
                    (narrow_hbm, narrow),
                    (row_hbm, row_twist),
                ]
            )
        ]
        for load in loads:
            load.start()
        pl.semaphore_wait(barrier, 13)

    half = STRIP // 2

    def piece(owner, rows, sems, slot, peer):
        return pltpu.make_async_remote_copy(
            src_ref=strip.at[owner, rows, :],
            dst_ref=strip.at[owner, rows, :],
            send_sem=sems[0].at[slot],
            recv_sem=sems[1].at[slot],
            device_id={"group": peer},
            device_id_type=MESH,
        )

    gather_sems, pass_sems = (gather_send, gather_recv), (pass_send, pass_recv)
    whole, top, bottom = pl.ds(0, STRIP), pl.ds(0, half), pl.ds(half, half)
    copies = []

    def send(*args):
        copies.append(piece(*args))
        copies[-1].start()

    def receive(*args):
        piece(*args).wait_recv()

    def screen(owner, rows=whole):
        for side_half in range(2):
            contrast = strip[owner, rows, pl.ds(HIGH * side_half, HIGH)]
            y1 = 2 * owner + side_half
            value = (incident[0, y1, rows, :], incident[1, y1, rows, :])
            value = cmul(sincos_small(contrast * (2.0 * math.pi * THICKNESS)), value)
            incident[0, y1, rows, :] = value[0]
            incident[1, y1, rows, :] = value[1]

    with jax.named_scope("gather_start"):
        loads[1].wait()
        send(group, whole, gather_sems, 0, group_next)
        send(group, whole, gather_sems, 1, group_last)
        send(group, whole, pass_sems, 0, partner)
        for peer in peers_y[:2]:
            signal(line_sem, "rows", peer)

    with jax.named_scope("incident_pupil"):
        loads[0].wait()
        tilt_row, tilt_col = tilts[0, 0], tilts[0, 1]
        pos_row = me * STRIP + lax.broadcasted_iota(jnp.int32, (STRIP, HIGH), 0)
        pos_col = lax.broadcasted_iota(jnp.int32, (STRIP, HIGH), 1)
        base = tilt_row * pos_row + tilt_col * pos_col
        for y1 in range(LOW):
            residue = (base + tilt_col * (HIGH * y1)) & (N - 1)
            cosine, sine = sincos_cycles(residue.astype(jnp.float32) * (1.0 / N))
            incident[0, y1] = cosine
            incident[1, y1] = sine

        lane = lax.broadcasted_iota(jnp.int32, (ROWS, FOLD * STRIP), 1)
        natural = lax.broadcasted_iota(jnp.int32, (ROWS, FOLD * STRIP), 0) + ROWS * lax.rem(lane, STRIP)
        freq_rows = jnp.where(natural < N // 2, natural, natural - N)
        tile_me = me // SLOTS
        slot_me = lax.rem(me, SLOTS)
        freq_cols = tile_me * FOLD + lane // STRIP + LOW * (slot_me * SUB - BANDS // 2)
        for sub in range(SUB):
            real, imag = pupil_parts(freq_rows, freq_cols + LOW * sub)
            pupil[0, sub] = real
            pupil[1, sub] = imag

    with jax.named_scope("gather_wait"):
        pl.semaphore_wait(line_sem, 2)
        for peer in peers_x:
            signal(plane_sem, "rows", peer)
        receive(group_last, whole, gather_sems, 0, group_next)
        send(group_last, top, gather_sems, 2, group_next)
        send(group_last, top, pass_sems, 3, other_next)
        send(group_last, whole, pass_sems, 1, partner)
        receive(group_next, whole, gather_sems, 1, group_last)
        send(group_next, bottom, gather_sems, 3, group_last)
        send(group_next, bottom, pass_sems, 4, other_last)
        send(group_next, whole, pass_sems, 2, partner)
        pl.semaphore_wait(plane_sem, 3)
        signal(pair_sem, "rows", peer_z)
        for owner in (group, group_last, group_next):
            screen(owner)
        receive(partner, whole, pass_sems, 0, partner)
        screen(partner)
        receive(group_far, top, gather_sems, 2, group_next)
        receive(group_far, bottom, gather_sems, 3, group_last)
        screen(group_far)
        for slot, (owner, rows) in enumerate([(other_last, whole), (other_next, whole)]):
            receive(owner, rows, pass_sems, 1 + slot, partner)
            screen(owner)
        for slot, rows in enumerate((top, bottom)):
            receive(other_far, rows, pass_sems, 3 + slot, partner)
        screen(other_far)
        for place in (2, 3, 4, 5):
            loads[place].wait()

    with jax.named_scope("screen_dft16"):
        for part in range(STRIP // 8):
            rows = pl.ds(8 * part, 8)
            values = []
            for y1 in range(LOW):
                values.append((incident[0, y1, rows, :], incident[1, y1, rows, :]))
            values = dft16(values, -1)
            for kap in range(LOW):
                twist = (col_twist[0, pl.ds(kap, 1), :], -col_twist[1, pl.ds(kap, 1), :])
                real, imag = cmul(values[kap], twist)
                place = pl.ds(kap * STRIP + 8 * part, 8)
                section[place, pl.ds(0, HIGH)] = real
                section[place, pl.ds(HIGH, HIGH)] = imag

    with jax.named_scope("column_128"):
        lanes = FOLD * STRIP
        tiles = [split(section[pl.ds(tile * lanes, lanes), :]) for tile in range(TILES)]

    side = lax.rem(group, 2)
    rows_y = {
        step: lax.rem(place_y + (1 - side) * step + side * (8 - step), 8) for step in (4, 3, 5, 2, 6, 1, 7, 0)
    }
    rows_x = {step: 8 * lax.rem(place_x + step, 4) for step in (2, 1, 3, 0)}
    rows_z = {1: 32 * (1 - place_z), 0: 32 * place_z}
    peers = [rows_y[y] + (rows_x[x] + rows_z[z]) for y in rows_y for x in rows_x for z in rows_z if x or y or z]

    def exchange(source, target, send_sem, recv_sem):
        msg = source.shape[0] // ROWS
        here = pl.ds(me * msg, msg)
        for peer in peers:
            pltpu.make_async_remote_copy(
                src_ref=source.at[pl.ds(peer * msg, msg), :],
                dst_ref=target.at[here, :],
                send_sem=send_sem,
                recv_sem=recv_sem,
                device_id={"rows": peer},
                device_id_type=MESH,
            ).start()
        target[pl.ds(me * msg, msg), :] = source[pl.ds(me * msg, msg), :]
        every = pl.ds(0, (ROWS - 1) * msg)
        return pltpu.make_async_remote_copy(
            src_ref=source.at[every, :],
            dst_ref=target.at[every, :],
            send_sem=send_sem,
            recv_sem=recv_sem,
            device_id={"rows": peer_z},
            device_id_type=MESH,
        )

    pl.semaphore_wait(pair_sem, 1)
    exchanges = []
    for chunk, (start, size) in enumerate(CHUNK_ROWS):
        with jax.named_scope("column_exchange"):
            forward = table(wide, (COL_FWD[0] + start, size))
            for tile in range(TILES):
                send_a[chunk][pl.ds(tile * size, size), :] = dot3(forward, tiles[tile], ((1,), (1,)))
            exchanges.append(exchange(send_a[chunk], recv_a[chunk], a_send.at[chunk], a_recv.at[chunk]))

    twist_cos, twist_sin = row_twist[0], row_twist[1]
    for chunk, (first, last) in enumerate(CHUNKS):
        subs = last - first
        msg = 2 * subs
        with jax.named_scope("row_wait"):
            exchanges[chunk].wait_recv()
        with jax.named_scope("row_work"):
            got = recv_a[chunk]
            parts = [
                jnp.concatenate([got[pl.ds(part * subs + sub, ROWS, stride=msg), :] for part in range(2)], axis=0)
                for sub in range(subs)
            ]
            data = split(jnp.concatenate(parts, axis=1))
            data = dot3(table(narrow, ROW_FWD), data, ((1,), (0,)))
            parts = []
            for sub in range(subs):
                columns = slice(sub * lanes, (sub + 1) * lanes)
                value = cmul((data[:ROWS, columns], data[ROWS:, columns]), (twist_cos, -twist_sin))
                parts.append(jnp.concatenate(value, axis=1))
            data = dot3(split(jnp.concatenate(parts, axis=0)), table(wide, IN_FWD), ((1,), (0,)))
            parts = []
            for sub in range(subs):
                rows = slice(sub * ROWS, (sub + 1) * ROWS)
                mask = (pupil[0, first + sub], pupil[1, first + sub])
                parts.append(jnp.concatenate(cmul((data[rows, :lanes], data[rows, lanes:]), mask), axis=1))
            data = dot3(split(jnp.concatenate(parts, axis=0)), table(wide, IN_INV), ((1,), (0,)))
            parts = []
            for sub in range(subs):
                rows = slice(sub * ROWS, (sub + 1) * ROWS)
                value = cmul((data[rows, :lanes], data[rows, lanes:]), (twist_cos, twist_sin))
                parts.append(jnp.concatenate(value, axis=0))
            data = dot3(table(narrow, ROW_INV), split(jnp.concatenate(parts, axis=1)), ((1,), (0,)))
            for sub in range(subs):
                columns = slice(sub * lanes, (sub + 1) * lanes)
                for part in range(2):
                    place = pl.ds(part * subs + sub, ROWS, stride=msg)
                    send_b[chunk][place, :] = data[part * ROWS : (part + 1) * ROWS, columns]
        with jax.named_scope("row_exchange"):
            exchanges.append(exchange(send_b[chunk], recv_b[chunk], b_send.at[chunk], b_recv.at[chunk]))

    for chunk, (start, size) in enumerate(CHUNK_ROWS):
        with jax.named_scope("column_wait"):
            exchanges[len(CHUNKS) + chunk].wait_recv()
        with jax.named_scope("columns_back"):
            inverse = table(wide, (COL_INV[0] + start, size))
            for tile in range(TILES):
                data = split(recv_b[chunk][pl.ds(tile * size, size), :].T)
                value = dot3(data, inverse, ((1,), (0,)))
                place = pl.ds(tile * lanes, lanes)
                section[place, :] = value if chunk == 0 else section[place, :] + value
    results = []
    with jax.named_scope("columns_last"):
        for part in range(STRIP // 8):
            values = []
            for kap in range(LOW):
                place = pl.ds(kap * STRIP + 8 * part, 8)
                twist = (col_twist[0, pl.ds(kap, 1), :], col_twist[1, pl.ds(kap, 1), :])
                values.append(cmul((section[place, pl.ds(0, HIGH)], section[place, pl.ds(HIGH, HIGH)]), twist))
            values = dft16(values, 1)
            for y1 in range(LOW):
                for plane in range(2):
                    out_ref[plane, pl.ds(8 * part, 8), pl.ds(HIGH * y1, HIGH)] = values[y1][plane]
            rows = pl.ds(8 * part, 8)
            results.append(pltpu.make_async_copy(out_ref.at[:, rows, :], out_hbm.at[:, rows, :], out_sems.at[part]))
            results[-1].start()

    for copy in copies + exchanges:
        copy.wait_send()
    for copy in results:
        copy.wait()


def per_device(illum_tilts, index_layers, measured):
    wide, narrow, col_twist, row_twist = tables()
    messages = [pltpu.VMEM((2 * (hi - lo) * ROWS, FOLD * STRIP), jnp.float32) for lo, hi in CHUNKS]
    field = pl.pallas_call(
        kernel,
        out_shape=jax.ShapeDtypeStruct((2, STRIP, N), jnp.float32),
        in_specs=[pl.BlockSpec(memory_space=pltpu.HBM)] * 6,
        out_specs=pl.BlockSpec(memory_space=pltpu.HBM),
        scratch_shapes=[
            pltpu.VMEM((GROUPS, STRIP, N // GROUPS), jnp.float32),
            pltpu.VMEM((2, LOW, STRIP, HIGH), jnp.float32),
            pltpu.VMEM((LOW * STRIP, 2 * HIGH), jnp.float32),
            messages,
            messages,
            messages,
            messages,
            pltpu.VMEM((2, SUB, ROWS, FOLD * STRIP), jnp.float32),
            pltpu.SMEM((1, 2), jnp.int32),
            pltpu.VMEM(wide.shape, jnp.bfloat16),
            pltpu.VMEM(narrow.shape, jnp.bfloat16),
            pltpu.VMEM(col_twist.shape, jnp.float32),
            pltpu.VMEM(row_twist.shape, jnp.float32),
            pltpu.VMEM((2, STRIP, N), jnp.float32),
            pltpu.SemaphoreType.DMA((STRIP // 8,)),
            pltpu.SemaphoreType.DMA((4,)),
            pltpu.SemaphoreType.DMA((4,)),
            pltpu.SemaphoreType.DMA((5,)),
            pltpu.SemaphoreType.DMA((5,)),
            pltpu.SemaphoreType.REGULAR,
            pltpu.SemaphoreType.REGULAR,
            pltpu.SemaphoreType.REGULAR,
            pltpu.SemaphoreType.DMA((len(CHUNKS),)),
            pltpu.SemaphoreType.DMA((len(CHUNKS),)),
            pltpu.SemaphoreType.DMA((len(CHUNKS),)),
            pltpu.SemaphoreType.DMA((len(CHUNKS),)),
            pltpu.SemaphoreType.DMA((6,)),
        ],
        compiler_params=pltpu.CompilerParams(
            collective_id=0, has_side_effects=True, vmem_limit_bytes=60 * 1024 * 1024
        ),
    )(
        illum_tilts,
        index_layers[0],
        jnp.asarray(wide),
        jnp.asarray(narrow),
        jnp.asarray(col_twist),
        jnp.asarray(row_twist),
    )
    return field[None] - measured


def solution(mesh):
    return jax.shard_map(
        per_device,
        mesh=mesh,
        in_specs=(P("group", None), P(None, "rows", "group"), P("group", None, "rows", None)),
        out_specs=P("group", None, "rows", None),
        check_vma=False,
    )
```
